32 devices in a mesh: sample: 2 (over y), space: 16 (over z, x, core).
Axes of the slice: x: 2, y: 2, z: 4, core: 2. Of those that a mesh axis runs over, the one named last changes fastest.
Arguments:
- volume: bfloat16 [32, 2, 32, 1024], P('space', 'sample'), may hold values from -6 to 6
- out_grads: bfloat16 [16, 2, 128, 256], P('space', 'sample'), may hold values from -6 to 6
- kernel_one: bfloat16 [27, 32, 64], replicated, may hold values from -0.21875 to 0.21875
- kernel_two: bfloat16 [27, 64, 128], replicated, may hold values from -0.15625 to 0.15625
Outputs:
- layer_out: bfloat16 [16, 2, 128, 256], P('space', 'sample')
- input_grads: bfloat16 [32, 2, 32, 1024], P('space', 'sample')
- kernel_one_grads: float32 [27, 32, 64], replicated
- kernel_two_grads: float32 [27, 64, 128], replicated
The draws below stay inside these ranges and needn't reach their ends.
All inputs are finite; a program needn't handle non-finite values.
Results may differ from the reference program's by a relative error of at most 0.015.
Values may be sent and summed in bfloat16 or wider, within the bound.
A program may use at most 128 MiB of HBM per device.

```python
import jax
import jax.numpy as jnp
from jax import lax

CIN = 32
C1 = 64
C2 = 128
SIDE = 32
Z = 32
BATCH = 2
PLANE = 1024
HALF = 16
Z2 = 16
PLANE2 = 256


def steps_of(stream_key, dims, shards, smallest, largest):
    def one(dim, shards_of):
        steps = jax.random.uniform(jax.random.fold_in(jax.random.fold_in(stream_key, 6), dim), (shards_of,), jnp.float32, smallest / len(shards), largest / len(shards))
        return jnp.repeat(jnp.exp(steps), dims[dim] // shards_of).reshape((-1,) + (1,) * (len(dims) - dim - 1))

    level = one(*shards[0])
    for cut in shards[1:]:
        level = level * one(*cut)
    return level


def bell_draw(key, extent, width, reach, shards=(), held_as=jnp.bfloat16):
    drawn = jax.random.normal(key, extent, jnp.float32) * width
    if len(shards) > 0:
        drawn = steps_of(key, extent, shards, -0.22, 0.18) * drawn
    return jnp.clip(drawn, min=-reach, max=reach).astype(held_as)


def setup_inputs(seed: int = 0) -> dict:
    splits = jax.random.split(jax.random.key(seed), 5)
    volume = bell_draw(splits[0], (Z, BATCH, CIN, PLANE), 1.0, 6.0, ((0, 16), (1, 2)))
    out_grads = bell_draw(splits[1], (Z2, BATCH, C2, PLANE2), 1.0, 6.0, ((0, 16), (1, 2)))
    kernel_one = bell_draw(splits[2], (27, CIN, C1), (27 * CIN) ** -0.5, 0.21875)
    kernel_two = bell_draw(splits[3], (27, C1, C2), (27 * C1) ** -0.5, 0.15625)
    return dict(volume=volume, out_grads=out_grads, kernel_one=kernel_one, kernel_two=kernel_two)


def convolve(inputs, kernel, stride):
    cube = kernel.reshape(3, 3, 3, kernel.shape[1], kernel.shape[2])
    return lax.conv_general_dilated(inputs, cube, (stride, stride, stride), [(1, 1), (1, 1), (1, 1)], dimension_numbers=('DNCHW', 'DHWIO', 'DNCHW'), precision=lax.Precision.HIGHEST)

def reference(volume, out_grads, kernel_one, kernel_two):
    cells = volume.astype(jnp.float32).reshape(Z, BATCH, CIN, SIDE, SIDE)
    first = kernel_one.astype(jnp.float32)
    second = kernel_two.astype(jnp.float32)
    pre_one, pull_one = jax.vjp(lambda inputs, kernel: convolve(inputs, kernel, 1), cells, first)
    hidden = lax.optimization_barrier(jax.nn.silu(pre_one).astype(jnp.bfloat16)).astype(jnp.float32)
    strided, pull_two = jax.vjp(lambda inputs, kernel: convolve(inputs, kernel, 2), hidden, second)
    layer_out = strided.astype(jnp.bfloat16).reshape(Z2, BATCH, C2, PLANE2)
    cotangent = out_grads.astype(jnp.float32).reshape(Z2, BATCH, C2, HALF, HALF)
    hidden_grads, kernel_two_grads = pull_two(cotangent)
    hidden_grads = lax.optimization_barrier(hidden_grads.astype(jnp.bfloat16)).astype(jnp.float32)
    sigma = jax.nn.sigmoid(pre_one)
    pre_grads = hidden_grads * sigma * (1.0 + pre_one * (1.0 - sigma))
    pre_grads = lax.optimization_barrier(pre_grads.astype(jnp.bfloat16)).astype(jnp.float32)
    input_grads, kernel_one_grads = pull_one(pre_grads)
    input_grads = input_grads.astype(jnp.bfloat16).reshape(Z, BATCH, CIN, PLANE)
    kernel_one_grads = kernel_one_grads * float(BATCH * Z * PLANE) ** (-0.5)
    kernel_two_grads = kernel_two_grads * float(BATCH * Z2 * PLANE2) ** (-0.5)
    return (layer_out, input_grads, kernel_one_grads, kernel_two_grads)
```

```python
import functools

import jax
import jax.numpy as jnp
from jax import lax
from jax.experimental import pallas as pl
from jax.experimental.pallas import tpu as pltpu
from jax.sharding import PartitionSpec as P

F32 = jnp.float32
BF16 = jnp.bfloat16
MESH = pl.DeviceIdType.MESH
VMEM_SPEC = pl.BlockSpec(memory_space=pltpu.VMEM)
PAIR = 14
ROWS_TWO = 27 * 64
ROWS_ONE = PAIR * 32
WINDOWS = {-1: (1, -1), 0: (0, 0), 1: (1, 0), 2: (0, 1)}


def group_sizes(samples, spaces):
    return 4 * samples, spaces // 4


def padded_rows(samples, spaces):
    first, second = group_sizes(samples, spaces)
    unit = first * second * 16
    return -(-(ROWS_TWO + ROWS_ONE) // unit) * unit


def mm(a, b, dims=((1,), (0,))):
    return lax.dot_general(a, b, (dims, ((), ())), preferred_element_type=F32)


def halo_kernel(spaces, vol, og, vlo, vhi, olo, ohi, send_sem, recv_sem):
    me = lax.axis_index("space")
    sample = lax.axis_index("sample")
    barrier = pltpu.get_barrier_semaphore()
    below, above = me - 1, me + 1

    @pl.when(me > 0)
    def _():
        pl.semaphore_signal(barrier, inc=1, device_id=(sample, below), device_id_type=MESH)

    @pl.when(me < spaces - 1)
    def _():
        pl.semaphore_signal(barrier, inc=1, device_id=(sample, above), device_id_type=MESH)

    pl.semaphore_wait(barrier, jnp.minimum(me, 1) + jnp.minimum(spaces - 1 - me, 1))

    def copy(src, dst, index, target):
        return pltpu.make_async_remote_copy(
            src_ref=src,
            dst_ref=dst,
            send_sem=send_sem.at[index],
            recv_sem=recv_sem.at[index],
            device_id=(sample, target),
            device_id_type=MESH,
        )

    up = [(vol, vlo, 0), (og, olo, 1)]
    down = [(vol, vhi, 2), (og, ohi, 3)]

    @pl.when(me < spaces - 1)
    def _():
        for src, dst, index in up:
            copy(src, dst, index, above).start()

    @pl.when(me > 0)
    def _():
        for src, dst, index in down:
            copy(src, dst, index, below).start()

    @pl.when(me < spaces - 1)
    def _():
        for src, dst, index in up:
            copy(src, dst, index, above).wait_send()
        for src, dst, index in down:
            copy(src, dst, index, above).wait_recv()

    @pl.when(me > 0)
    def _():
        for src, dst, index in down:
            copy(src, dst, index, below).wait_send()
        for src, dst, index in up:
            copy(src, dst, index, below).wait_recv()


def windows(parts, lanes, us):
    cell = lax.broadcasted_iota(jnp.int32, (1, lanes), 1)
    q, r = (cell >> 4) & 15, cell & 15
    for uy in us:
        for ux in us:
            (py, sy), (px, sx) = WINDOWS[uy], WINDOWS[ux]
            part = parts(2 * py + px)
            offset = 16 * sy + sx
            if offset != 0:
                part = pltpu.roll(part, (-offset) % lanes, 1)
                inside = (q + sy >= 0) & (q + sy <= 15) & (r + sx >= 0) & (r + sx <= 15)
                part = jnp.where(inside, part, 0.0)
            yield part.astype(BF16)


def tap_block(kernel, dz, dy, dx, shape):
    if 0 <= dy <= 2 and 0 <= dx <= 2:
        return kernel[9 * dz + 3 * dy + dx]
    return jnp.zeros(shape, BF16)


def math_kernel(
    spaces, vol, vlo, vhi, og, olo, ohi, k1, k2,
    layer, igrads, grads,
    order, t1, t2, o4, tg, w1, wb, wc, hgrads,
):
    me = lax.axis_index("space")
    has_low, has_high = me > 0, me < spaces - 1

    def order_rows(step, carry):
        start = pl.multiple_of(step * 128, 128)
        col = lax.broadcasted_iota(jnp.int32, (1, 1024), 1)
        phase, q, r = col >> 8, (col >> 4) & 15, col & 15
        source = (2 * q + (phase >> 1)) * 32 + 2 * r + (phase & 1)
        row = lax.broadcasted_iota(jnp.int32, (128, 1024), 0) + start
        order[pl.ds(start, 128), :] = jnp.where(row == source, 1.0, 0.0).astype(BF16)
        return carry

    lax.fori_loop(0, 8, order_rows, 0)

    us = (-1, 0, 1, 2)
    phases = [(0, 0), (0, 1), (1, 0), (1, 1)]
    for dz in range(3):
        for index, (uy, ux) in enumerate((a, b) for a in us for b in us):
            w1[dz, 32 * index : 32 * index + 32, :] = jnp.concatenate(
                [tap_block(k1, dz, uy - py + 1, ux - px + 1, (32, 64)) for py, px in phases], axis=1
            )
        for index, (py, px) in enumerate(phases):
            wc[dz, 32 * index : 32 * index + 32, :] = jnp.concatenate(
                [tap_block(k1, dz, py + 1 - uy, px + 1 - ux, (32, 64)) for uy in us for ux in us],
                axis=1,
            )
            taps = {(0, 0): 1, (0, 1): -1, (1, 0): 2, (1, 1): 0}
            wb[dz, 64 * index : 64 * index + 64, :] = jnp.concatenate(
                [
                    tap_block(k2, dz, taps[py, sy], taps[px, sx], (64, 128))
                    for sy in (0, 1)
                    for sx in (0, 1)
                ],
                axis=1,
            )

    zero = jnp.zeros((), BF16)
    low = jnp.where(has_low, vlo[...].reshape(64, 1024), zero)
    high = jnp.where(has_high, vhi[...].reshape(64, 1024), zero)
    cells = jnp.concatenate([low, vol[...].reshape(64, 1024), high], axis=0)
    split = mm(cells, order[...])

    def volume_part(phase):
        return jnp.concatenate(
            [split[32 * p : 32 * p + 32, 256 * phase : 256 * phase + 256] for p in range(6)], axis=1
        )

    for index, part in enumerate(windows(volume_part, 1536, us)):
        t1[32 * index : 32 * index + 32, :] = part

    og_three = jnp.concatenate(
        [jnp.where(has_low, olo[...], zero), og[...], jnp.where(has_high, ohi[...], zero)], axis=1
    ).astype(F32)
    cell = lax.broadcasted_iota(jnp.int32, (1, 768), 1)
    q, r = (cell >> 4) & 15, cell & 15
    for sy in (0, 1):
        for sx in (0, 1):
            part = og_three
            if sy + sx > 0:
                part = pltpu.roll(part, 768 - 16 * sy - sx, 1)
                part = jnp.where((q + sy <= 15) & (r + sx <= 15), part, 0.0)
            index = 2 * sy + sx
            o4[128 * index : 128 * index + 128, :] = part.astype(BF16)

    even = mm(wb[1], o4[:, 256:768])
    odd = mm(wb[2], o4[:, 0:512]) + mm(wb[0], o4[:, 256:768])
    hgrads[:, 0:256] = odd[:, 0:256].astype(BF16)
    hgrads[:, 256:512] = even[:, 0:256].astype(BF16)
    hgrads[:, 512:768] = odd[:, 256:512].astype(BF16)
    hgrads[:, 768:1024] = even[:, 256:512].astype(BF16)

    tn = ((0,), (0,))
    nt = ((1,), (1,))
    pre = mm(w1[0], t1[:, 0:1024], tn)
    pre += mm(w1[1], t1[:, 256:1280], tn)
    pre += mm(w1[2], t1[:, 512:1536], tn)
    sigma = 1.0 / (1.0 + jnp.exp(-pre))
    plane = lax.broadcasted_iota(jnp.int32, (1, 1024), 1) >> 8
    real = ((plane > 0) | has_low) & ((plane < 3) | has_high)
    hidden = jnp.where(real, pre * sigma, 0.0).astype(BF16).astype(F32)
    slope = hgrads[...].astype(F32) * sigma * (1.0 + pre * (1.0 - sigma))
    pre_grads = jnp.where(real, slope, 0.0).astype(BF16)
    pre_wide = pre_grads.astype(F32)

    for index, part in enumerate(
        windows(lambda ph: hidden[64 * ph : 64 * ph + 64, 0:768], 768, (-1, 0, 1))
    ):
        t2[64 * index : 64 * index + 64, :] = part
    total = jnp.zeros((128, 256), F32)
    for dz in range(3):
        here = t2[:, 256 * dz : 256 * dz + 256]
        total += mm(k2[9 * dz : 9 * dz + 9].reshape(576, 128), here, tn)
        grads[576 * dz : 576 * dz + 576, :] = mm(here, og[...], nt).astype(BF16)
    layer[...] = total.astype(BF16)

    pairs = {}
    for dz in range(3):
        here = mm(t1[:, 256 * dz + 256 : 256 * dz + 768], pre_grads[:, 256:768], nt)
        for dy in range(3):
            for dx in range(3):
                term = None
                for index, (py, px) in enumerate(phases):
                    row = 32 * (4 * (py + dy) + px + dx)
                    block = here[row : row + 32, 64 * index : 64 * index + 64]
                    term = block if term is None else term + block
                pairs[9 * dz + 3 * dy + dx] = term
    pairs[27] = jnp.zeros((32, 64), F32)
    for tap in range(PAIR):
        grads[ROWS_TWO + 32 * tap : ROWS_TWO + 32 * tap + 32, :] = jnp.concatenate(
            [pairs[tap], pairs[tap + PAIR]], axis=1
        ).astype(BF16)
    used = ROWS_TWO + ROWS_ONE
    if grads.shape[0] > used:
        grads[used:, :] = jnp.zeros((grads.shape[0] - used, 128), BF16)

    for index, part in enumerate(
        windows(lambda ph: pre_wide[64 * ph : 64 * ph + 64, :], 1024, us)
    ):
        tg[64 * index : 64 * index + 64, :] = part
    back = mm(wc[0], tg[:, 512:1024]) + mm(wc[1], tg[:, 256:768]) + mm(wc[2], tg[:, 0:512])
    back = back.astype(BF16)
    for z in range(2):
        plane_rows = jnp.concatenate(
            [back[32 * ph : 32 * ph + 32, 256 * z : 256 * z + 256] for ph in range(4)], axis=1
        )
        igrads[z] = mm(plane_rows, order[...], nt).astype(BF16)


def reduce_kernel(samples, spaces, grads, out, slots_a, part, slots_b, sems):
    sample, space = lax.axis_index("sample"), lax.axis_index("space")
    size_a, size_b = group_sizes(samples, spaces)
    chunk_a = out.shape[0] // size_a
    chunk_b = chunk_a // size_b
    mine_a = sample * 4 + lax.rem(space, 4)
    mine_b = space // 4

    def peer_a(member):
        return (member // 4, mine_b * 4 + lax.rem(member, 4))

    def peer_b(member):
        return (sample, member * 4 + lax.rem(space, 4))

    others_a = [lax.rem(mine_a + d, size_a) for d in range(size_a)]
    others_b = [lax.rem(mine_b + d, size_b) for d in range(size_b)]
    barrier = pltpu.get_barrier_semaphore()
    for d in range(1, size_a):
        pl.semaphore_signal(barrier, inc=1, device_id=peer_a(others_a[d]), device_id_type=MESH)
    for d in range(1, size_b):
        pl.semaphore_signal(barrier, inc=1, device_id=peer_b(others_b[d]), device_id_type=MESH)
    pl.semaphore_wait(barrier, size_a + size_b - 2)

    def rows_a(member):
        return pl.ds(pl.multiple_of(member * chunk_a, 16), chunk_a)

    def rows_b(member):
        return pl.ds(pl.multiple_of(member * chunk_b, 16), chunk_b)

    def exchange(stage, count, make):
        copies = []
        for d in range(1, count):
            src, dst, target = make(d)
            copies.append(
                pltpu.make_async_remote_copy(
                    src_ref=src,
                    dst_ref=dst,
                    send_sem=sems.at[0, stage, d],
                    recv_sem=sems.at[1, stage, d],
                    device_id=target,
                    device_id_type=MESH,
                )
            )
        for item in copies:
            item.start()
        return copies

    def finish(copies):
        for item in copies:
            item.wait()

    finish(
        exchange(
            0,
            size_a,
            lambda d: (grads.at[rows_a(others_a[d])], slots_a.at[d], peer_a(others_a[d])),
        )
    )
    total = grads[rows_a(mine_a), :].astype(F32)
    for d in range(1, size_a):
        total += slots_a[d].astype(F32)
    part[...] = total.astype(BF16)
    finish(
        exchange(
            1,
            size_b,
            lambda d: (part.at[rows_b(others_b[d])], slots_b.at[d], peer_b(others_b[d])),
        )
    )
    total = part[rows_b(mine_b), :].astype(F32)
    for d in range(1, size_b):
        total += slots_b[d].astype(F32)
    here = pl.ds(pl.multiple_of(mine_a * chunk_a + mine_b * chunk_b, 16), chunk_b)
    out[here, :] = total.astype(BF16)
    finish(
        exchange(2, size_b, lambda d: (out.at[here], out.at[here], peer_b(others_b[d])))
    )
    whole = rows_a(mine_a)
    finish(
        exchange(3, size_a, lambda d: (out.at[whole], out.at[whole], peer_a(others_a[d])))
    )


def local(volume, out_grads, kernel_one, kernel_two):
    spaces, samples = lax.axis_size("space"), lax.axis_size("sample")
    depth, batch, channels_in, plane = volume.shape
    scale_one = float(samples * batch * spaces * depth * plane) ** (-0.5)
    scale_two = scale_one * 8.0**0.5
    vol = volume.reshape(depth, channels_in, plane)
    og = out_grads.reshape(128, 256)
    any_spec = pl.BlockSpec(memory_space=pl.ANY)
    vlo, vhi, olo, ohi = pl.pallas_call(
        functools.partial(halo_kernel, spaces),
        out_shape=[jax.ShapeDtypeStruct(a.shape, a.dtype) for a in (vol, vol, og, og)],
        in_specs=[any_spec] * 2,
        out_specs=[any_spec] * 4,
        scratch_shapes=[pltpu.SemaphoreType.DMA((4,)), pltpu.SemaphoreType.DMA((4,))],
        compiler_params=pltpu.CompilerParams(collective_id=0, has_side_effects=True),
        name="halo",
    )(vol, og)
    rows = padded_rows(samples, spaces)
    layer, igrads, grads = pl.pallas_call(
        functools.partial(math_kernel, spaces),
        out_shape=[
            jax.ShapeDtypeStruct((128, 256), BF16),
            jax.ShapeDtypeStruct((2, 32, 1024), BF16),
            jax.ShapeDtypeStruct((rows, 128), BF16),
        ],
        in_specs=[VMEM_SPEC] * 8,
        out_specs=[VMEM_SPEC] * 3,
        scratch_shapes=[
            pltpu.VMEM((1024, 1024), BF16),
            pltpu.VMEM((512, 1536), BF16),
            pltpu.VMEM((576, 768), BF16),
            pltpu.VMEM((512, 768), BF16),
            pltpu.VMEM((1024, 1024), BF16),
            pltpu.VMEM((3, 512, 256), BF16),
            pltpu.VMEM((3, 256, 512), BF16),
            pltpu.VMEM((3, 128, 1024), BF16),
            pltpu.VMEM((256, 1024), BF16),
        ],
        compiler_params=pltpu.CompilerParams(vmem_limit_bytes=48 * 2**20),
        name="conv_pair",
    )(vol, vlo, vhi, og, olo, ohi, kernel_one, kernel_two)
    size_a, size_b = group_sizes(samples, spaces)
    summed = pl.pallas_call(
        functools.partial(reduce_kernel, samples, spaces),
        out_shape=jax.ShapeDtypeStruct((rows, 128), BF16),
        in_specs=[VMEM_SPEC],
        out_specs=VMEM_SPEC,
        scratch_shapes=[
            pltpu.VMEM((size_a, rows // size_a, 128), BF16),
            pltpu.VMEM((rows // size_a, 128), BF16),
            pltpu.VMEM((size_b, rows // size_a // size_b, 128), BF16),
            pltpu.SemaphoreType.DMA((2, 4, max(size_a, size_b))),
        ],
        compiler_params=pltpu.CompilerParams(
            collective_id=1, has_side_effects=True, vmem_limit_bytes=32 * 2**20
        ),
        name="sum_all",
    )(grads)
    second = summed[:ROWS_TWO].reshape(27, 64, 128).astype(F32) * scale_two
    pair = summed[ROWS_TWO : ROWS_TWO + ROWS_ONE].reshape(PAIR, 32, 128)
    first = jnp.concatenate([pair[:, :, :64], pair[:-1, :, 64:]], axis=0).astype(F32) * scale_one
    return (
        layer.reshape(1, 1, 128, 256),
        igrads.reshape(volume.shape),
        first,
        second,
    )


def solution(mesh):
    in_specs = (P("space", "sample", None, None), P("space", "sample", None, None), P(), P())
    out_specs = (P("space", "sample", None, None), P("space", "sample", None, None), P(), P())
    return jax.shard_map(local, mesh=mesh, in_specs=in_specs, out_specs=out_specs, check_vma=False)
```

```python
import functools

import jax
import jax.numpy as jnp
from jax import lax
from jax.experimental import pallas as pl
from jax.experimental.pallas import tpu as pltpu
from jax.sharding import PartitionSpec as P

F32 = jnp.float32
BF16 = jnp.bfloat16
MESH = pl.DeviceIdType.MESH
VMEM_SPEC = pl.BlockSpec(memory_space=pltpu.VMEM)
PAIR = 14
ROWS_TWO = 27 * 64
ROWS_ONE = PAIR * 32
WINDOWS = {-1: (1, -1), 0: (0, 0), 1: (1, 0), 2: (0, 1)}


def plan(samples, spaces):
    chips, lines = 2 * samples, spaces // 4
    unit = 2 * chips * 16
    rows = -(-(ROWS_TWO + ROWS_ONE) // unit) * unit
    early = ROWS_TWO // unit * unit
    return chips, lines, ((0, early), (early, rows - early))


def line_rows(size, chips, lines):
    return -(-(size // 2 // chips) // lines // 16) * 16


def mm(a, b, dims=((1,), (0,))):
    return lax.dot_general(a, b, (dims, ((), ())), preferred_element_type=F32)


def windows(parts, lanes, us):
    cell = lax.broadcasted_iota(jnp.int32, (1, lanes), 1)
    q, r = (cell >> 4) & 15, cell & 15
    for uy in us:
        for ux in us:
            (py, sy), (px, sx) = WINDOWS[uy], WINDOWS[ux]
            part = parts(2 * py + px)
            offset = 16 * sy + sx
            if offset != 0:
                part = pltpu.roll(part, (-offset) % lanes, 1)
                inside = (q + sy >= 0) & (q + sy <= 15) & (r + sx >= 0) & (r + sx <= 15)
                part = jnp.where(inside, part, 0.0)
            yield part.astype(BF16)


def tap_block(kernel, dz, dy, dx, shape):
    if 0 <= dy <= 2 and 0 <= dx <= 2:
        return kernel[9 * dz + 3 * dy + dx]
    return jnp.zeros(shape, BF16)


class Sum:
    def __init__(self, stream, base, size, samples, spaces, grads, out, bufs, sems):
        self.stream, self.base = stream, base
        self.grads, self.out, self.bufs, self.sems = grads, out, bufs, sems
        self.chips, self.lines = 2 * samples, spaces // 4
        sample, space = lax.axis_index("sample"), lax.axis_index("space")
        core, line = lax.rem(space, 2), space // 4
        chip = 2 * sample + lax.rem(space // 2, 2)
        self.core, self.chip, self.line = core, chip, line
        self.half = size // 2
        self.chunk = self.half // self.chips
        self.part = line_rows(size, self.chips, self.lines)
        self.sibling = (sample, space + 1 - 2 * core)
        self.others = [lax.rem(chip + d, self.chips) for d in range(self.chips)]
        self.chip_peers = [(c // 2, 4 * line + 2 * lax.rem(c, 2) + core) for c in self.others]
        self.ahead = [lax.rem(line + d, self.lines) for d in range(self.lines)]
        self.line_peers = [(sample, 4 * n + lax.rem(space, 4)) for n in self.ahead]
        self.flying = []

    def peers(self):
        return [self.sibling] + self.chip_peers[1:] + self.line_peers[1:]

    def rows(self, start, size):
        return pl.ds(pl.multiple_of(start, 16), size)

    def send(self, stage, items):
        self.flying = []
        for d, (src, dst, target) in enumerate(items):
            copy = pltpu.make_async_remote_copy(
                src_ref=src,
                dst_ref=dst,
                send_sem=self.sems.at[0, self.stream, stage, d],
                recv_sem=self.sems.at[1, self.stream, stage, d],
                device_id=target,
                device_id_type=MESH,
            )
            copy.start()
            self.flying.append(copy)

    def wait(self):
        for copy in self.flying:
            copy.wait()

    def pair(self):
        slot = self.bufs[0]
        away = self.rows(self.base + (1 - self.core) * self.half, self.half)
        self.send(0, [(self.grads.at[away], slot, self.sibling)])

    def plane(self):
        self.wait()
        slot, held, slots = self.bufs[0], self.bufs[1], self.bufs[2]
        own = self.grads[self.rows(self.base + self.core * self.half, self.half), :]
        held[...] = (own.astype(F32) + slot[...].astype(F32)).astype(BF16)
        items = []
        for d in range(1, self.chips):
            src = held.at[self.rows(self.others[d] * self.chunk, self.chunk)]
            items.append((src, slots.at[d], self.chip_peers[d]))
        self.send(1, items)

    def line_sum(self):
        self.wait()
        held, slots, part, far = self.bufs[1], self.bufs[2], self.bufs[3], self.bufs[4]
        total = held[self.rows(self.chip * self.chunk, self.chunk), :].astype(F32)
        for d in range(1, self.chips):
            total += slots[d].astype(F32)
        part[0 : self.chunk, :] = total.astype(BF16)
        extra = part.shape[0] - self.chunk
        if extra > 0:
            part[self.chunk :, :] = jnp.zeros((extra, 128), BF16)
        items = []
        for d in range(1, self.lines):
            src = part.at[self.rows(self.ahead[d] * self.part, self.part)]
            items.append((src, far.at[d], self.line_peers[d]))
        self.send(2, items)

    def line_back(self):
        self.wait()
        part, far, done = self.bufs[3], self.bufs[4], self.bufs[5]
        mine = self.rows(self.line * self.part, self.part)
        total = part[mine, :].astype(F32)
        for d in range(1, self.lines):
            total += far[d].astype(F32)
        done[mine, :] = total.astype(BF16)
        items = []
        for d in range(1, self.lines):
            items.append((done.at[mine], done.at[mine], self.line_peers[d]))
        self.send(3, items)

    def plane_back(self):
        self.wait()
        start = self.base + self.core * self.half + self.chip * self.chunk
        mine = self.rows(start, self.chunk)
        self.out[mine, :] = self.bufs[5][0 : self.chunk, :]
        items = []
        for d in range(1, self.chips):
            items.append((self.out.at[mine], self.out.at[mine], self.chip_peers[d]))
        self.send(4, items)

    def pair_back(self):
        self.wait()
        mine = self.rows(self.base + self.core * self.half, self.half)
        self.send(5, [(self.out.at[mine], self.out.at[mine], self.sibling)])


def whole_kernel(
    samples, spaces, vol_far, og_far, k1_far, k2_far,
    layer, igrads, out,
    vol, og, k1, k2, vlo, vhi, olo, ohi, grads,
    order, t1, t2, o4, tg, w1, wb, wc, hgrads,
    *rest,
):
    sems, local_sems, halo_sems = rest[12:]
    me, sample = lax.axis_index("space"), lax.axis_index("sample")
    has_low, has_high = me > 0, me < spaces - 1
    below, above = me - 1, me + 1
    fetched = [
        pltpu.make_async_copy(src, dst, local_sems.at[n])
        for n, (src, dst) in enumerate(
            [(k1_far, k1), (k2_far, k2), (vol_far, vol), (og_far, og)]
        )
    ]
    for item in fetched:
        item.start()

    _, _, streams = plan(samples, spaces)
    first, second = [
        Sum(n, base, size, samples, spaces, grads, out, rest[6 * n : 6 * n + 6], sems)
        for n, (base, size) in enumerate(streams)
    ]
    barrier = pltpu.get_barrier_semaphore()

    @pl.when(has_low)
    def _():
        pl.semaphore_signal(barrier, inc=1, device_id=(sample, below), device_id_type=MESH)

    @pl.when(has_high)
    def _():
        pl.semaphore_signal(barrier, inc=1, device_id=(sample, above), device_id_type=MESH)

    peers = first.peers()
    for peer in peers:
        pl.semaphore_signal(barrier, inc=1, device_id=peer, device_id_type=MESH)
    near = jnp.minimum(me, 1) + jnp.minimum(spaces - 1 - me, 1)
    pl.semaphore_wait(barrier, near + len(peers))

    def halo(src, dst, index, target):
        return pltpu.make_async_remote_copy(
            src_ref=src,
            dst_ref=dst,
            send_sem=halo_sems.at[0, index],
            recv_sem=halo_sems.at[1, index],
            device_id=(sample, target),
            device_id_type=MESH,
        )

    up = [(vol_far, vlo, 0), (og_far, olo, 1)]
    down = [(vol_far, vhi, 2), (og_far, ohi, 3)]

    @pl.when(has_high)
    def _():
        for src, dst, index in up:
            halo(src, dst, index, above).start()

    @pl.when(has_low)
    def _():
        for src, dst, index in down:
            halo(src, dst, index, below).start()

    def order_rows(step, carry):
        start = pl.multiple_of(step * 128, 128)
        col = lax.broadcasted_iota(jnp.int32, (1, 1024), 1)
        phase, q, r = col >> 8, (col >> 4) & 15, col & 15
        source = (2 * q + (phase >> 1)) * 32 + 2 * r + (phase & 1)
        row = lax.broadcasted_iota(jnp.int32, (128, 1024), 0) + start
        order[pl.ds(start, 128), :] = jnp.where(row == source, 1.0, 0.0).astype(BF16)
        return carry

    lax.fori_loop(0, 8, order_rows, 0)

    fetched[0].wait()
    fetched[1].wait()
    us = (-1, 0, 1, 2)
    phases = [(0, 0), (0, 1), (1, 0), (1, 1)]
    for dz in range(3):
        for index, (uy, ux) in enumerate((a, b) for a in us for b in us):
            w1[dz, 32 * index : 32 * index + 32, :] = jnp.concatenate(
                [tap_block(k1, dz, uy - py + 1, ux - px + 1, (32, 64)) for py, px in phases], axis=1
            )
        for index, (py, px) in enumerate(phases):
            wc[dz, 32 * index : 32 * index + 32, :] = jnp.concatenate(
                [tap_block(k1, dz, py + 1 - uy, px + 1 - ux, (32, 64)) for uy in us for ux in us],
                axis=1,
            )
            taps = {(0, 0): 1, (0, 1): -1, (1, 0): 2, (1, 1): 0}
            wb[dz, 64 * index : 64 * index + 64, :] = jnp.concatenate(
                [
                    tap_block(k2, dz, taps[py, sy], taps[px, sx], (64, 128))
                    for sy in (0, 1)
                    for sx in (0, 1)
                ],
                axis=1,
            )

    fetched[2].wait()
    fetched[3].wait()

    @pl.when(has_high)
    def _():
        for src, dst, index in up:
            halo(src, dst, index, above).wait_send()
        for src, dst, index in down:
            halo(src, dst, index, above).wait_recv()

    @pl.when(has_low)
    def _():
        for src, dst, index in down:
            halo(src, dst, index, below).wait_send()
        for src, dst, index in up:
            halo(src, dst, index, below).wait_recv()

    zero = jnp.zeros((), BF16)
    low = jnp.where(has_low, vlo[...].reshape(64, 1024), zero)
    high = jnp.where(has_high, vhi[...].reshape(64, 1024), zero)
    cells = jnp.concatenate([low, vol[...].reshape(64, 1024), high], axis=0)
    split = mm(cells, order[...])

    def volume_part(phase):
        return jnp.concatenate(
            [split[32 * p : 32 * p + 32, 256 * phase : 256 * phase + 256] for p in range(6)], axis=1
        )

    for index, part in enumerate(windows(volume_part, 1536, us)):
        t1[32 * index : 32 * index + 32, :] = part

    tn = ((0,), (0,))
    nt = ((1,), (1,))
    pre = mm(w1[0], t1[:, 0:1024], tn)
    pre += mm(w1[1], t1[:, 256:1280], tn)
    pre += mm(w1[2], t1[:, 512:1536], tn)
    sigma = 1.0 / (1.0 + jnp.exp(-pre))
    plane = lax.broadcasted_iota(jnp.int32, (1, 1024), 1) >> 8
    real = ((plane > 0) | has_low) & ((plane < 3) | has_high)
    hidden = jnp.where(real, pre * sigma, 0.0).astype(BF16).astype(F32)
    for index, part in enumerate(
        windows(lambda ph: hidden[64 * ph : 64 * ph + 64, 0:768], 768, (-1, 0, 1))
    ):
        t2[64 * index : 64 * index + 64, :] = part
    for dz in range(3):
        here = t2[:, 256 * dz : 256 * dz + 256]
        grads[576 * dz : 576 * dz + 576, :] = mm(here, og[...], nt).astype(BF16)
    first.pair()

    og_three = jnp.concatenate(
        [jnp.where(has_low, olo[...], zero), og[...], jnp.where(has_high, ohi[...], zero)], axis=1
    ).astype(F32)
    cell = lax.broadcasted_iota(jnp.int32, (1, 768), 1)
    q, r = (cell >> 4) & 15, cell & 15
    for sy in (0, 1):
        for sx in (0, 1):
            part = og_three
            if sy + sx > 0:
                part = pltpu.roll(part, 768 - 16 * sy - sx, 1)
                part = jnp.where((q + sy <= 15) & (r + sx <= 15), part, 0.0)
            index = 2 * sy + sx
            o4[128 * index : 128 * index + 128, :] = part.astype(BF16)

    even = mm(wb[1], o4[:, 256:768])
    odd = mm(wb[2], o4[:, 0:512]) + mm(wb[0], o4[:, 256:768])
    hgrads[:, 0:256] = odd[:, 0:256].astype(BF16)
    hgrads[:, 256:512] = even[:, 0:256].astype(BF16)
    hgrads[:, 512:768] = odd[:, 256:512].astype(BF16)
    hgrads[:, 768:1024] = even[:, 256:512].astype(BF16)

    slope = hgrads[...].astype(F32) * sigma * (1.0 + pre * (1.0 - sigma))
    pre_grads = jnp.where(real, slope, 0.0).astype(BF16)
    pre_wide = pre_grads.astype(F32)

    pairs = {}
    for dz in range(3):
        here = mm(t1[:, 256 * dz + 256 : 256 * dz + 768], pre_grads[:, 256:768], nt)
        for dy in range(3):
            for dx in range(3):
                term = None
                for index, (py, px) in enumerate(phases):
                    row = 32 * (4 * (py + dy) + px + dx)
                    block = here[row : row + 32, 64 * index : 64 * index + 64]
                    term = block if term is None else term + block
                pairs[9 * dz + 3 * dy + dx] = term
    pairs[27] = jnp.zeros((32, 64), F32)
    for tap in range(PAIR):
        grads[ROWS_TWO + 32 * tap : ROWS_TWO + 32 * tap + 32, :] = jnp.concatenate(
            [pairs[tap], pairs[tap + PAIR]], axis=1
        ).astype(BF16)
    used = ROWS_TWO + ROWS_ONE
    if grads.shape[0] > used:
        grads[used:, :] = jnp.zeros((grads.shape[0] - used, 128), BF16)
    second.pair()
    first.plane()

    total = jnp.zeros((128, 256), F32)
    for dz in range(3):
        here = t2[:, 256 * dz : 256 * dz + 256]
        total += mm(k2[9 * dz : 9 * dz + 9].reshape(576, 128), here, tn)
    layer[...] = total.astype(BF16)

    for index, part in enumerate(
        windows(lambda ph: pre_wide[64 * ph : 64 * ph + 64, :], 1024, us)
    ):
        tg[64 * index : 64 * index + 64, :] = part
    second.plane()

    back = mm(wc[0], tg[:, 512:1024]) + mm(wc[1], tg[:, 256:768]) + mm(wc[2], tg[:, 0:512])
    back = back.astype(BF16)
    for z in range(2):
        plane_rows = jnp.concatenate(
            [back[32 * ph : 32 * ph + 32, 256 * z : 256 * z + 256] for ph in range(4)], axis=1
        )
        igrads[z] = mm(plane_rows, order[...], nt).astype(BF16)

    first.line_sum()
    second.line_sum()
    first.line_back()
    second.line_back()
    first.plane_back()
    second.plane_back()
    first.pair_back()
    second.pair_back()
    first.wait()
    second.wait()


def local(volume, out_grads, kernel_one, kernel_two):
    spaces, samples = lax.axis_size("space"), lax.axis_size("sample")
    depth, batch, channels_in, plane = volume.shape
    scale_one = float(samples * batch * spaces * depth * plane) ** (-0.5)
    scale_two = scale_one * 8.0**0.5
    vol = volume.reshape(depth, channels_in, plane)
    og = out_grads.reshape(128, 256)
    chips, lines, streams = plan(samples, spaces)
    rows = streams[1][0] + streams[1][1]
    buffers = []
    for _, size in streams:
        half, chunk = size // 2, size // 2 // chips
        part = line_rows(size, chips, lines)
        buffers += [
            pltpu.VMEM((half, 128), BF16),
            pltpu.VMEM((half, 128), BF16),
            pltpu.VMEM((chips, chunk, 128), BF16),
            pltpu.VMEM((lines * part, 128), BF16),
            pltpu.VMEM((lines, part, 128), BF16),
            pltpu.VMEM((lines * part, 128), BF16),
        ]
    layer, igrads, summed = pl.pallas_call(
        functools.partial(whole_kernel, samples, spaces),
        out_shape=[
            jax.ShapeDtypeStruct((128, 256), BF16),
            jax.ShapeDtypeStruct((2, 32, 1024), BF16),
            jax.ShapeDtypeStruct((rows, 128), BF16),
        ],
        in_specs=[pl.BlockSpec(memory_space=pl.ANY)] * 4,
        out_specs=[VMEM_SPEC] * 3,
        scratch_shapes=[
            pltpu.VMEM(vol.shape, BF16),
            pltpu.VMEM(og.shape, BF16),
            pltpu.VMEM(kernel_one.shape, BF16),
            pltpu.VMEM(kernel_two.shape, BF16),
            pltpu.VMEM(vol.shape, BF16),
            pltpu.VMEM(vol.shape, BF16),
            pltpu.VMEM(og.shape, BF16),
            pltpu.VMEM(og.shape, BF16),
            pltpu.VMEM((rows, 128), BF16),
            pltpu.VMEM((1024, 1024), BF16),
            pltpu.VMEM((512, 1536), BF16),
            pltpu.VMEM((576, 768), BF16),
            pltpu.VMEM((512, 768), BF16),
            pltpu.VMEM((1024, 1024), BF16),
            pltpu.VMEM((3, 512, 256), BF16),
            pltpu.VMEM((3, 256, 512), BF16),
            pltpu.VMEM((3, 128, 1024), BF16),
            pltpu.VMEM((256, 1024), BF16),
            *buffers,
            pltpu.SemaphoreType.DMA((2, 2, 6, max(chips, lines))),
            pltpu.SemaphoreType.DMA((4,)),
            pltpu.SemaphoreType.DMA((2, 4)),
        ],
        compiler_params=pltpu.CompilerParams(
            collective_id=0, has_side_effects=True, vmem_limit_bytes=56 * 2**20
        ),
        name="conv_pair",
    )(vol, og, kernel_one, kernel_two)
    second = summed[:ROWS_TWO].reshape(27, 64, 128).astype(F32) * scale_two
    pair = summed[ROWS_TWO : ROWS_TWO + ROWS_ONE].reshape(PAIR, 32, 128)
    first = jnp.concatenate([pair[:, :, :64], pair[:-1, :, 64:]], axis=0).astype(F32) * scale_one
    return (
        layer.reshape(1, 1, 128, 256),
        igrads.reshape(volume.shape),
        first,
        second,
    )


def solution(mesh):
    in_specs = (P("space", "sample", None, None), P("space", "sample", None, None), P(), P())
    out_specs = (P("space", "sample", None, None), P("space", "sample", None, None), P(), P())
    return jax.shard_map(local, mesh=mesh, in_specs=in_specs, out_specs=out_specs, check_vma=False)
```

```python
import functools

import jax
import jax.numpy as jnp
from jax import lax
from jax.experimental import pallas as pl
from jax.experimental.pallas import tpu as pltpu
from jax.sharding import PartitionSpec as P

F32 = jnp.float32
BF16 = jnp.bfloat16
MESH = pl.DeviceIdType.MESH
VMEM_SPEC = pl.BlockSpec(memory_space=pltpu.VMEM)
PAIR = 14
ROWS_TWO = 27 * 64
ROWS_ONE = PAIR * 32
WINDOWS = {-1: (1, -1), 0: (0, 0), 1: (1, 0), 2: (0, 1)}


def plan(samples, spaces):
    chips, lines = 2 * samples, spaces // 4
    unit = 2 * chips * 16
    rows = -(-(ROWS_TWO + ROWS_ONE) // unit) * unit
    early = ROWS_TWO // unit * unit
    return chips, lines, ((0, early), (early, rows - early))


def line_rows(size, chips, lines):
    return -(-(size // 2 // chips) // lines // 16) * 16


def mm(a, b, dims=((1,), (0,))):
    return lax.dot_general(a, b, (dims, ((), ())), preferred_element_type=F32)


def windows(parts, lanes, us):
    cell = lax.broadcasted_iota(jnp.int32, (1, lanes), 1)
    q, r = (cell >> 4) & 15, cell & 15
    for uy in us:
        for ux in us:
            (py, sy), (px, sx) = WINDOWS[uy], WINDOWS[ux]
            part = parts(2 * py + px)
            offset = 16 * sy + sx
            if offset != 0:
                part = pltpu.roll(part, (-offset) % lanes, 1)
                inside = (q + sy >= 0) & (q + sy <= 15) & (r + sx >= 0) & (r + sx <= 15)
                part = jnp.where(inside, part, 0.0)
            yield part.astype(BF16)


def tap_block(kernel, dz, dy, dx, shape):
    if 0 <= dy <= 2 and 0 <= dx <= 2:
        return kernel[9 * dz + 3 * dy + dx]
    return jnp.zeros(shape, BF16)


class Sum:
    def __init__(self, base, size, samples, spaces, grads, out, bufs, sems):
        self.base = base
        self.grads, self.out, self.bufs, self.sems = grads, out, bufs, sems
        self.chips, self.lines = 2 * samples, spaces // 4
        sample, space = lax.axis_index("sample"), lax.axis_index("space")
        core, line = lax.rem(space, 2), space // 4
        chip = 2 * sample + lax.rem(space // 2, 2)
        self.core, self.chip, self.line = core, chip, line
        self.half = size // 2
        self.chunk = self.half // self.chips
        self.part = line_rows(size, self.chips, self.lines)
        self.sibling = (sample, space + 1 - 2 * core)
        self.others = [lax.rem(chip + d, self.chips) for d in range(self.chips)]
        self.chip_peers = [(c // 2, 4 * line + 2 * lax.rem(c, 2) + core) for c in self.others]
        self.ahead = [lax.rem(line + d, self.lines) for d in range(self.lines)]
        self.line_peers = [(sample, 4 * n + lax.rem(space, 4)) for n in self.ahead]
        self.flying = []

    def rows(self, start, size):
        return pl.ds(pl.multiple_of(start, 16), size)

    def send(self, stage, items):
        self.flying = []
        for d, (src, dst, target) in enumerate(items):
            copy = pltpu.make_async_remote_copy(
                src_ref=src,
                dst_ref=dst,
                send_sem=self.sems.at[0, stage, d],
                recv_sem=self.sems.at[1, stage, d],
                device_id=target,
                device_id_type=MESH,
            )
            copy.start()
            self.flying.append(copy)

    def wait(self):
        for copy in self.flying:
            copy.wait()

    def pair(self):
        slot = self.bufs[0]
        away = self.rows(self.base + (1 - self.core) * self.half, self.half)
        self.send(0, [(self.grads.at[away], slot, self.sibling)])

    def plane(self):
        self.wait()
        slot, held, slots = self.bufs[0], self.bufs[1], self.bufs[2]
        own = self.grads[self.rows(self.base + self.core * self.half, self.half), :]
        held[...] = (own.astype(F32) + slot[...].astype(F32)).astype(BF16)
        items = []
        for d in range(1, self.chips):
            src = held.at[self.rows(self.others[d] * self.chunk, self.chunk)]
            items.append((src, slots.at[d], self.chip_peers[d]))
        self.send(1, items)

    def line_sum(self):
        self.wait()
        held, slots, part, far = self.bufs[1], self.bufs[2], self.bufs[3], self.bufs[4]
        total = held[self.rows(self.chip * self.chunk, self.chunk), :].astype(F32)
        for d in range(1, self.chips):
            total += slots[d].astype(F32)
        part[0 : self.chunk, :] = total.astype(BF16)
        extra = part.shape[0] - self.chunk
        if extra > 0:
            part[self.chunk :, :] = jnp.zeros((extra, 128), BF16)
        items = []
        for d in range(1, self.lines):
            src = part.at[self.rows(self.ahead[d] * self.part, self.part)]
            items.append((src, far.at[d], self.line_peers[d]))
        self.send(2, items)

    def line_back(self):
        self.wait()
        part, far, done = self.bufs[3], self.bufs[4], self.bufs[5]
        mine = self.rows(self.line * self.part, self.part)
        total = part[mine, :].astype(F32)
        for d in range(1, self.lines):
            total += far[d].astype(F32)
        done[mine, :] = total.astype(BF16)
        items = []
        for d in range(1, self.lines):
            items.append((done.at[mine], done.at[mine], self.line_peers[d]))
        self.send(3, items)

    def plane_back(self):
        self.wait()
        start = self.base + self.core * self.half + self.chip * self.chunk
        mine = self.rows(start, self.chunk)
        self.out[mine, :] = self.bufs[5][0 : self.chunk, :]
        items = []
        for d in range(1, self.chips):
            items.append((self.out.at[mine], self.out.at[mine], self.chip_peers[d]))
        self.send(4, items)

    def pair_back(self):
        self.wait()
        mine = self.rows(self.base + self.core * self.half, self.half)
        self.send(5, [(self.out.at[mine], self.out.at[mine], self.sibling)])


class QuickSum:
    def __init__(self, first, base, size, grads, out, bufs, sems):
        self.first, self.base, self.grads, self.out, self.bufs = first, base, grads, out, bufs
        self.sems = sems
        self.members = 2 * first.chips
        self.chunk = size // self.members
        me = 2 * first.chip + first.core
        self.mine = first.rows(base + me * self.chunk, self.chunk)
        self.others = [lax.rem(me + d, self.members) for d in range(self.members)]
        self.peers = [
            (m // 4, 4 * first.line + 2 * lax.rem(m // 2, 2) + lax.rem(m, 2)) for m in self.others
        ]

    def send(self, stage, items):
        self.flying = []
        for d, (src, dst, target) in enumerate(items):
            copy = pltpu.make_async_remote_copy(
                src_ref=src,
                dst_ref=dst,
                send_sem=self.sems.at[0, stage, d],
                recv_sem=self.sems.at[1, stage, d],
                device_id=target,
                device_id_type=MESH,
            )
            copy.start()
            self.flying.append(copy)

    def wait(self):
        for copy in self.flying:
            copy.wait()

    def plane(self):
        items = []
        for d in range(1, self.members):
            away = self.first.rows(self.base + self.others[d] * self.chunk, self.chunk)
            items.append((self.grads.at[away], self.bufs[0].at[d], self.peers[d]))
        self.send(0, items)

    def line(self):
        self.wait()
        slots, held = self.bufs
        total = self.grads[self.mine, :].astype(F32)
        for d in range(1, self.members):
            total += slots[d].astype(F32)
        here = self.first.rows(self.first.line * self.chunk, self.chunk)
        held[here, :] = total.astype(BF16)
        target = held.at[here]
        self.send(1, [(target, target, peer) for peer in self.first.line_peers[1:]])

    def back(self):
        self.wait()
        held = self.bufs[1]
        total = held[0 : self.chunk, :].astype(F32)
        for n in range(1, self.first.lines):
            total += held[n * self.chunk : (n + 1) * self.chunk, :].astype(F32)
        self.out[self.mine, :] = total.astype(BF16)
        target = self.out.at[self.mine]
        self.send(2, [(target, target, peer) for peer in self.peers[1:]])


def whole_kernel(
    samples, spaces, vol_far, og_far, k1_far, k2_far,
    layer, igrads, out,
    vol, og, k1, k2, vlo, vhi, olo, ohi, grads,
    order, t1, t2, o4, tg, w1, wb, wc, hgrads,
    *rest,
):
    sems, quick_sems, local_sems, halo_sems = rest[8:]
    me, sample = lax.axis_index("space"), lax.axis_index("sample")
    has_low, has_high = me > 0, me < spaces - 1
    below, above = me - 1, me + 1
    fetched = [
        pltpu.make_async_copy(src, dst, local_sems.at[n])
        for n, (src, dst) in enumerate(
            [(k1_far, k1), (k2_far, k2), (vol_far, vol), (og_far, og)]
        )
    ]
    for item in fetched:
        item.start()

    _, _, streams = plan(samples, spaces)
    first = Sum(*streams[0], samples, spaces, grads, out, rest[0:6], sems)
    second = QuickSum(first, *streams[1], grads, out, rest[6:8], quick_sems)
    barrier = pltpu.get_barrier_semaphore()

    @pl.when(has_low)
    def _():
        pl.semaphore_signal(barrier, inc=1, device_id=(sample, below), device_id_type=MESH)

    @pl.when(has_high)
    def _():
        pl.semaphore_signal(barrier, inc=1, device_id=(sample, above), device_id_type=MESH)

    peers = second.peers[1:] + first.line_peers[1:]
    for peer in peers:
        pl.semaphore_signal(barrier, inc=1, device_id=peer, device_id_type=MESH)
    near = jnp.minimum(me, 1) + jnp.minimum(spaces - 1 - me, 1)
    pl.semaphore_wait(barrier, near + len(peers))

    def halo(src, dst, index, target):
        return pltpu.make_async_remote_copy(
            src_ref=src,
            dst_ref=dst,
            send_sem=halo_sems.at[0, index],
            recv_sem=halo_sems.at[1, index],
            device_id=(sample, target),
            device_id_type=MESH,
        )

    up = [(og_far, olo, 0), (vol_far, vlo, 1)]
    down = [(og_far, ohi, 2), (vol_far, vhi, 3)]

    @pl.when(has_high)
    def _():
        for src, dst, index in up:
            halo(src, dst, index, above).start()

    @pl.when(has_low)
    def _():
        for src, dst, index in down:
            halo(src, dst, index, below).start()

    def order_rows(step, carry):
        start = pl.multiple_of(step * 128, 128)
        col = lax.broadcasted_iota(jnp.int32, (1, 1024), 1)
        phase, q, r = col >> 8, (col >> 4) & 15, col & 15
        source = (2 * q + (phase >> 1)) * 32 + 2 * r + (phase & 1)
        row = lax.broadcasted_iota(jnp.int32, (128, 1024), 0) + start
        order[pl.ds(start, 128), :] = jnp.where(row == source, 1.0, 0.0).astype(BF16)
        return carry

    lax.fori_loop(0, 8, order_rows, 0)

    fetched[0].wait()
    fetched[1].wait()
    us = (-1, 0, 1, 2)
    phases = [(0, 0), (0, 1), (1, 0), (1, 1)]
    for dz in range(3):
        for index, (uy, ux) in enumerate((a, b) for a in us for b in us):
            w1[dz, 32 * index : 32 * index + 32, :] = jnp.concatenate(
                [tap_block(k1, dz, uy - py + 1, ux - px + 1, (32, 64)) for py, px in phases], axis=1
            )
        for index, (py, px) in enumerate(phases):
            wc[dz, 32 * index : 32 * index + 32, :] = jnp.concatenate(
                [tap_block(k1, dz, py + 1 - uy, px + 1 - ux, (32, 64)) for uy in us for ux in us],
                axis=1,
            )
            taps = {(0, 0): 1, (0, 1): -1, (1, 0): 2, (1, 1): 0}
            wb[dz, 64 * index : 64 * index + 64, :] = jnp.concatenate(
                [
                    tap_block(k2, dz, taps[py, sy], taps[px, sx], (64, 128))
                    for sy in (0, 1)
                    for sx in (0, 1)
                ],
                axis=1,
            )

    def arrive(n):
        @pl.when(has_high)
        def _():
            src, dst, index = up[n]
            halo(src, dst, index, above).wait_send()
            src, dst, index = down[n]
            halo(src, dst, index, above).wait_recv()

        @pl.when(has_low)
        def _():
            src, dst, index = down[n]
            halo(src, dst, index, below).wait_send()
            src, dst, index = up[n]
            halo(src, dst, index, below).wait_recv()

    fetched[2].wait()
    fetched[3].wait()
    arrive(0)
    zero = jnp.zeros((), BF16)
    og_three = jnp.concatenate(
        [jnp.where(has_low, olo[...], zero), og[...], jnp.where(has_high, ohi[...], zero)], axis=1
    ).astype(F32)
    cell = lax.broadcasted_iota(jnp.int32, (1, 768), 1)
    q, r = (cell >> 4) & 15, cell & 15
    for sy in (0, 1):
        for sx in (0, 1):
            part = og_three
            if sy + sx > 0:
                part = pltpu.roll(part, 768 - 16 * sy - sx, 1)
                part = jnp.where((q + sy <= 15) & (r + sx <= 15), part, 0.0)
            index = 2 * sy + sx
            o4[128 * index : 128 * index + 128, :] = part.astype(BF16)

    even = mm(wb[1], o4[:, 256:768])
    odd = mm(wb[2], o4[:, 0:512]) + mm(wb[0], o4[:, 256:768])
    hgrads[:, 0:256] = odd[:, 0:256].astype(BF16)
    hgrads[:, 256:512] = even[:, 0:256].astype(BF16)
    hgrads[:, 512:768] = odd[:, 256:512].astype(BF16)
    hgrads[:, 768:1024] = even[:, 256:512].astype(BF16)
    arrive(1)
    low = jnp.where(has_low, vlo[...].reshape(64, 1024), zero)
    high = jnp.where(has_high, vhi[...].reshape(64, 1024), zero)
    cells = jnp.concatenate([low, vol[...].reshape(64, 1024), high], axis=0)
    split = mm(cells, order[...])

    def volume_part(phase):
        return jnp.concatenate(
            [split[32 * p : 32 * p + 32, 256 * phase : 256 * phase + 256] for p in range(6)], axis=1
        )

    for index, part in enumerate(windows(volume_part, 1536, us)):
        t1[32 * index : 32 * index + 32, :] = part

    tn = ((0,), (0,))
    nt = ((1,), (1,))
    pre = mm(w1[0], t1[:, 0:1024], tn)
    pre += mm(w1[1], t1[:, 256:1280], tn)
    pre += mm(w1[2], t1[:, 512:1536], tn)
    sigma = 1.0 / (1.0 + jnp.exp(-pre))
    plane = lax.broadcasted_iota(jnp.int32, (1, 1024), 1) >> 8
    real = ((plane > 0) | has_low) & ((plane < 3) | has_high)
    hidden = jnp.where(real, pre * sigma, 0.0).astype(BF16).astype(F32)
    for index, part in enumerate(
        windows(lambda ph: hidden[64 * ph : 64 * ph + 64, 0:768], 768, (-1, 0, 1))
    ):
        t2[64 * index : 64 * index + 64, :] = part
    for dz in range(3):
        here = t2[:, 256 * dz : 256 * dz + 256]
        grads[576 * dz : 576 * dz + 576, :] = mm(here, og[...], nt).astype(BF16)
    first.pair()

    total = jnp.zeros((128, 256), F32)
    for dz in range(3):
        here = t2[:, 256 * dz : 256 * dz + 256]
        total += mm(k2[9 * dz : 9 * dz + 9].reshape(576, 128), here, tn)
    layer[...] = total.astype(BF16)

    slope = hgrads[...].astype(F32) * sigma * (1.0 + pre * (1.0 - sigma))
    pre_grads = jnp.where(real, slope, 0.0).astype(BF16)
    pre_wide = pre_grads.astype(F32)

    first.plane()

    pairs = {}
    for dz in range(3):
        here = mm(t1[:, 256 * dz + 256 : 256 * dz + 768], pre_grads[:, 256:768], nt)
        for dy in range(3):
            for dx in range(3):
                term = None
                for index, (py, px) in enumerate(phases):
                    row = 32 * (4 * (py + dy) + px + dx)
                    block = here[row : row + 32, 64 * index : 64 * index + 64]
                    term = block if term is None else term + block
                pairs[9 * dz + 3 * dy + dx] = term
    pairs[27] = jnp.zeros((32, 64), F32)
    for tap in range(PAIR):
        grads[ROWS_TWO + 32 * tap : ROWS_TWO + 32 * tap + 32, :] = jnp.concatenate(
            [pairs[tap], pairs[tap + PAIR]], axis=1
        ).astype(BF16)
    used = ROWS_TWO + ROWS_ONE
    if grads.shape[0] > used:
        grads[used:, :] = jnp.zeros((grads.shape[0] - used, 128), BF16)
    second.plane()

    for index, part in enumerate(
        windows(lambda ph: pre_wide[64 * ph : 64 * ph + 64, :], 1024, us)
    ):
        tg[64 * index : 64 * index + 64, :] = part
    back = mm(wc[0], tg[:, 512:1024]) + mm(wc[1], tg[:, 256:768]) + mm(wc[2], tg[:, 0:512])
    back = back.astype(BF16)
    for z in range(2):
        plane_rows = jnp.concatenate(
            [back[32 * ph : 32 * ph + 32, 256 * z : 256 * z + 256] for ph in range(4)], axis=1
        )
        igrads[z] = mm(plane_rows, order[...], nt).astype(BF16)

    first.line_sum()
    second.line()
    first.line_back()
    second.back()
    first.plane_back()
    first.pair_back()
    second.wait()
    first.wait()


def tail_kernel(scale_one, scale_two, layer, igrads, summed, layer_out, igrads_out, first, second):
    layer_out[...] = layer[...]
    igrads_out[...] = igrads[...]
    second[...] = summed[0:ROWS_TWO, :].astype(F32) * scale_two
    for tap in range(27):
        start = ROWS_TWO + 32 * (tap % PAIR)
        block = summed[start : start + 32, :]
        half = block[:, 0:64] if tap < PAIR else block[:, 64:128]
        first[tap] = half.astype(F32) * scale_one


def local(volume, out_grads, kernel_one, kernel_two):
    spaces, samples = lax.axis_size("space"), lax.axis_size("sample")
    depth, batch, channels_in, plane = volume.shape
    scale_one = float(samples * batch * spaces * depth * plane) ** (-0.5)
    scale_two = scale_one * 8.0**0.5
    vol = volume.reshape(depth, channels_in, plane)
    og = out_grads.reshape(128, 256)
    chips, lines, streams = plan(samples, spaces)
    rows = streams[1][0] + streams[1][1]
    early, late = streams[0][1], streams[1][1]
    half, chunk = early // 2, early // 2 // chips
    part, quick = line_rows(early, chips, lines), late // 2 // chips
    layer, igrads, summed = pl.pallas_call(
        functools.partial(whole_kernel, samples, spaces),
        out_shape=[
            jax.ShapeDtypeStruct((128, 256), BF16),
            jax.ShapeDtypeStruct((2, 32, 1024), BF16),
            jax.ShapeDtypeStruct((rows, 128), BF16),
        ],
        in_specs=[pl.BlockSpec(memory_space=pltpu.HBM)] * 4,
        out_specs=[VMEM_SPEC] * 3,
        scratch_shapes=[
            pltpu.VMEM(vol.shape, BF16),
            pltpu.VMEM(og.shape, BF16),
            pltpu.VMEM(kernel_one.shape, BF16),
            pltpu.VMEM(kernel_two.shape, BF16),
            pltpu.VMEM(vol.shape, BF16),
            pltpu.VMEM(vol.shape, BF16),
            pltpu.VMEM(og.shape, BF16),
            pltpu.VMEM(og.shape, BF16),
            pltpu.VMEM((rows, 128), BF16),
            pltpu.VMEM((1024, 1024), BF16),
            pltpu.VMEM((512, 1536), BF16),
            pltpu.VMEM((576, 768), BF16),
            pltpu.VMEM((512, 768), BF16),
            pltpu.VMEM((1024, 1024), BF16),
            pltpu.VMEM((3, 512, 256), BF16),
            pltpu.VMEM((3, 256, 512), BF16),
            pltpu.VMEM((3, 128, 1024), BF16),
            pltpu.VMEM((256, 1024), BF16),
            pltpu.VMEM((half, 128), BF16),
            pltpu.VMEM((half, 128), BF16),
            pltpu.VMEM((chips, chunk, 128), BF16),
            pltpu.VMEM((lines * part, 128), BF16),
            pltpu.VMEM((lines, part, 128), BF16),
            pltpu.VMEM((lines * part, 128), BF16),
            pltpu.VMEM((2 * chips, quick, 128), BF16),
            pltpu.VMEM((lines * quick, 128), BF16),
            pltpu.SemaphoreType.DMA((2, 6, max(chips, lines))),
            pltpu.SemaphoreType.DMA((2, 3, max(2 * chips, lines))),
            pltpu.SemaphoreType.DMA((4,)),
            pltpu.SemaphoreType.DMA((2, 4)),
        ],
        compiler_params=pltpu.CompilerParams(
            collective_id=0, has_side_effects=True, vmem_limit_bytes=56 * 2**20
        ),
        name="conv_pair",
    )(vol, og, kernel_one, kernel_two)
    layer, igrads, first, second = pl.pallas_call(
        functools.partial(tail_kernel, scale_one, scale_two),
        out_shape=[
            jax.ShapeDtypeStruct(layer.shape, BF16),
            jax.ShapeDtypeStruct(igrads.shape, BF16),
            jax.ShapeDtypeStruct(kernel_one.shape, F32),
            jax.ShapeDtypeStruct((ROWS_TWO, 128), F32),
        ],
        in_specs=[VMEM_SPEC] * 3,
        out_specs=[VMEM_SPEC] * 4,
        compiler_params=pltpu.CompilerParams(vmem_limit_bytes=56 * 2**20),
        name="finish",
    )(layer, igrads, summed)
    return (
        layer.reshape(out_grads.shape),
        igrads.reshape(volume.shape),
        first,
        second.reshape(kernel_two.shape),
    )


def solution(mesh):
    in_specs = (P("space", "sample", None, None), P("space", "sample", None, None), P(), P())
    out_specs = (P("space", "sample", None, None), P("space", "sample", None, None), P(), P())
    return jax.shard_map(local, mesh=mesh, in_specs=in_specs, out_specs=out_specs, check_vma=False)
```

```python
import functools
import math

import jax
import jax.numpy as jnp
from jax import lax
from jax.experimental import pallas as pl
from jax.experimental.pallas import tpu as pltpu
from jax.sharding import PartitionSpec as P

F32 = jnp.float32
BF16 = jnp.bfloat16
MESH = pl.DeviceIdType.MESH
VMEM_SPEC = pl.BlockSpec(memory_space=pltpu.VMEM)
PAIR = 14
ROWS_TWO = 27 * 64
ROWS_ONE = PAIR * 32
WINDOWS = {-1: (1, -1), 0: (0, 0), 1: (1, 0), 2: (0, 1)}


def plan(samples, spaces):
    chips, lines = 2 * samples, spaces // 4
    unit = 32 * math.lcm(chips, lines)
    units = -(-(ROWS_TWO + ROWS_ONE) // unit)
    early = ROWS_TWO // unit
    cut = (early + 1) // 2
    bounds = [0, cut * unit, early * unit, units * unit]
    streams = [(bounds[n], bounds[n + 1] - bounds[n], n == 1) for n in range(3)]
    return chips, lines, streams


def level_rows(size, outer, inner):
    chunk = size // 2 // outer
    return chunk, -(-chunk // inner // 16) * 16


def mm(a, b, dims=((1,), (0,))):
    return lax.dot_general(a, b, (dims, ((), ())), preferred_element_type=F32)


def windows(parts, lanes, us):
    cell = lax.broadcasted_iota(jnp.int32, (1, lanes), 1)
    q, r = (cell >> 4) & 15, cell & 15
    for uy in us:
        for ux in us:
            (py, sy), (px, sx) = WINDOWS[uy], WINDOWS[ux]
            part = parts(2 * py + px)
            offset = 16 * sy + sx
            if offset != 0:
                part = pltpu.roll(part, (-offset) % lanes, 1)
                inside = (q + sy >= 0) & (q + sy <= 15) & (r + sx >= 0) & (r + sx <= 15)
                part = jnp.where(inside, part, 0.0)
            yield part.astype(BF16)


def tap_block(kernel, dz, dy, dx, shape):
    if 0 <= dy <= 2 and 0 <= dx <= 2:
        return kernel[9 * dz + 3 * dy + dx]
    return jnp.zeros(shape, BF16)


class Sum:
    def __init__(self, stream, samples, spaces, grads, out, bufs, sems):
        self.base, size, line_first = stream
        self.grads, self.out, self.sems = grads, out, sems
        self.slot, self.held, self.slots, self.part, self.far, self.done = bufs
        chips, lines = 2 * samples, spaces // 4
        sample, space = lax.axis_index("sample"), lax.axis_index("space")
        core, line = lax.rem(space, 2), space // 4
        chip = 2 * sample + lax.rem(space // 2, 2)
        self.core, self.half = core, size // 2
        self.sibling = (sample, space + 1 - 2 * core)
        others = [lax.rem(chip + d, chips) for d in range(chips)]
        ahead = [lax.rem(line + d, lines) for d in range(lines)]
        plane = (chip, others, [(c // 2, 4 * line + 2 * lax.rem(c, 2) + core) for c in others])
        column = (line, ahead, [(sample, 4 * n + lax.rem(space, 4)) for n in ahead])
        self.outer, self.inner = (column, plane) if line_first else (plane, column)
        self.chunk, self.piece = level_rows(size, len(self.outer[1]), len(self.inner[1]))

    def peers(self):
        return [self.sibling] + self.outer[2][1:] + self.inner[2][1:]

    def rows(self, start, size):
        return pl.ds(pl.multiple_of(start, 16), size)

    def send(self, stage, items):
        self.flying = []
        for d, (src, dst, target) in enumerate(items):
            copy = pltpu.make_async_remote_copy(
                src_ref=src,
                dst_ref=dst,
                send_sem=self.sems.at[0, stage, d],
                recv_sem=self.sems.at[1, stage, d],
                device_id=target,
                device_id_type=MESH,
            )
            copy.start()
            self.flying.append(copy)

    def wait(self):
        for copy in self.flying:
            copy.wait()

    def scatter(self, stage, level, source, size, slots):
        _, indices, peers = level
        items = []
        for d in range(1, len(peers)):
            src = source.at[self.rows(indices[d] * size, size)]
            items.append((src, slots.at[d], peers[d]))
        self.send(stage, items)

    def gathered(self, level, source, size, slots):
        total = source[self.rows(level[0] * size, size), :].astype(F32)
        for d in range(1, len(level[2])):
            total += slots[d].astype(F32)
        return total.astype(BF16)

    def pair(self):
        away = self.rows(self.base + (1 - self.core) * self.half, self.half)
        self.send(0, [(self.grads.at[away], self.slot, self.sibling)])

    def first_level(self):
        self.wait()
        own = self.grads[self.rows(self.base + self.core * self.half, self.half), :]
        self.held[...] = (own.astype(F32) + self.slot[...].astype(F32)).astype(BF16)
        self.scatter(1, self.outer, self.held, self.chunk, self.slots)

    def second_level(self):
        self.wait()
        self.part[0 : self.chunk, :] = self.gathered(self.outer, self.held, self.chunk, self.slots)
        extra = self.part.shape[0] - self.chunk
        if extra > 0:
            self.part[self.chunk :, :] = jnp.zeros((extra, 128), BF16)
        self.scatter(2, self.inner, self.part, self.piece, self.far)

    def second_back(self):
        self.wait()
        mine = self.rows(self.inner[0] * self.piece, self.piece)
        self.done[mine, :] = self.gathered(self.inner, self.part, self.piece, self.far)
        target = self.done.at[mine]
        self.send(3, [(target, target, peer) for peer in self.inner[2][1:]])

    def first_back(self):
        self.wait()
        start = self.base + self.core * self.half + self.outer[0] * self.chunk
        mine = self.rows(start, self.chunk)
        self.out[mine, :] = self.done[0 : self.chunk, :]
        target = self.out.at[mine]
        self.send(4, [(target, target, peer) for peer in self.outer[2][1:]])

    def pair_back(self):
        self.wait()
        target = self.out.at[self.rows(self.base + self.core * self.half, self.half)]
        self.send(5, [(target, target, self.sibling)])


def whole_kernel(
    samples, spaces, vol_far, og_far, k1_far, k2_far,
    layer, igrads, out,
    vol, og, k1, k2, vlo, vhi, olo, ohi, grads,
    order, t1, t2, o4, tg, w1, wb, wc, hgrads,
    *rest,
):
    sems, local_sems, halo_sems = rest[18:]
    me, sample = lax.axis_index("space"), lax.axis_index("sample")
    has_low, has_high = me > 0, me < spaces - 1
    below, above = me - 1, me + 1
    fetched = [
        pltpu.make_async_copy(src, dst, local_sems.at[n])
        for n, (src, dst) in enumerate(
            [(k1_far, k1), (k2_far, k2), (vol_far, vol), (og_far, og)]
        )
    ]
    for item in fetched:
        item.start()

    _, _, streams = plan(samples, spaces)
    sums = [
        Sum(stream, samples, spaces, grads, out, rest[6 * n : 6 * n + 6], sems.at[n])
        for n, stream in enumerate(streams)
    ]
    first, second, late = sums
    barrier = pltpu.get_barrier_semaphore()

    @pl.when(has_low)
    def _():
        pl.semaphore_signal(barrier, inc=1, device_id=(sample, below), device_id_type=MESH)

    @pl.when(has_high)
    def _():
        pl.semaphore_signal(barrier, inc=1, device_id=(sample, above), device_id_type=MESH)

    peers = first.peers()
    for peer in peers:
        pl.semaphore_signal(barrier, inc=1, device_id=peer, device_id_type=MESH)
    near = jnp.minimum(me, 1) + jnp.minimum(spaces - 1 - me, 1)
    pl.semaphore_wait(barrier, near + len(peers))

    def halo(src, dst, index, target):
        return pltpu.make_async_remote_copy(
            src_ref=src,
            dst_ref=dst,
            send_sem=halo_sems.at[0, index],
            recv_sem=halo_sems.at[1, index],
            device_id=(sample, target),
            device_id_type=MESH,
        )

    up = [(og_far, olo, 0), (vol_far, vlo, 1)]
    down = [(og_far, ohi, 2), (vol_far, vhi, 3)]

    @pl.when(has_high)
    def _():
        for src, dst, index in up:
            halo(src, dst, index, above).start()

    @pl.when(has_low)
    def _():
        for src, dst, index in down:
            halo(src, dst, index, below).start()

    def order_rows(step, carry):
        start = pl.multiple_of(step * 128, 128)
        col = lax.broadcasted_iota(jnp.int32, (1, 1024), 1)
        phase, q, r = col >> 8, (col >> 4) & 15, col & 15
        source = (2 * q + (phase >> 1)) * 32 + 2 * r + (phase & 1)
        row = lax.broadcasted_iota(jnp.int32, (128, 1024), 0) + start
        order[pl.ds(start, 128), :] = jnp.where(row == source, 1.0, 0.0).astype(BF16)
        return carry

    lax.fori_loop(0, 8, order_rows, 0)

    fetched[0].wait()
    fetched[1].wait()
    us = (-1, 0, 1, 2)
    phases = [(0, 0), (0, 1), (1, 0), (1, 1)]
    for dz in range(3):
        for index, (uy, ux) in enumerate((a, b) for a in us for b in us):
            w1[dz, 32 * index : 32 * index + 32, :] = jnp.concatenate(
                [tap_block(k1, dz, uy - py + 1, ux - px + 1, (32, 64)) for py, px in phases], axis=1
            )
        for index, (py, px) in enumerate(phases):
            wc[dz, 32 * index : 32 * index + 32, :] = jnp.concatenate(
                [tap_block(k1, dz, py + 1 - uy, px + 1 - ux, (32, 64)) for uy in us for ux in us],
                axis=1,
            )
            taps = {(0, 0): 1, (0, 1): -1, (1, 0): 2, (1, 1): 0}
            wb[dz, 64 * index : 64 * index + 64, :] = jnp.concatenate(
                [
                    tap_block(k2, dz, taps[py, sy], taps[px, sx], (64, 128))
                    for sy in (0, 1)
                    for sx in (0, 1)
                ],
                axis=1,
            )

    def arrive(n):
        @pl.when(has_high)
        def _():
            src, dst, index = up[n]
            halo(src, dst, index, above).wait_send()
            src, dst, index = down[n]
            halo(src, dst, index, above).wait_recv()

        @pl.when(has_low)
        def _():
            src, dst, index = down[n]
            halo(src, dst, index, below).wait_send()
            src, dst, index = up[n]
            halo(src, dst, index, below).wait_recv()

    fetched[2].wait()
    fetched[3].wait()
    arrive(0)
    zero = jnp.zeros((), BF16)
    og_three = jnp.concatenate(
        [jnp.where(has_low, olo[...], zero), og[...], jnp.where(has_high, ohi[...], zero)], axis=1
    ).astype(F32)
    cell = lax.broadcasted_iota(jnp.int32, (1, 768), 1)
    q, r = (cell >> 4) & 15, cell & 15
    for sy in (0, 1):
        for sx in (0, 1):
            part = og_three
            if sy + sx > 0:
                part = pltpu.roll(part, 768 - 16 * sy - sx, 1)
                part = jnp.where((q + sy <= 15) & (r + sx <= 15), part, 0.0)
            index = 2 * sy + sx
            o4[128 * index : 128 * index + 128, :] = part.astype(BF16)

    even = mm(wb[1], o4[:, 256:768])
    odd = mm(wb[2], o4[:, 0:512]) + mm(wb[0], o4[:, 256:768])
    hgrads[:, 0:256] = odd[:, 0:256].astype(BF16)
    hgrads[:, 256:512] = even[:, 0:256].astype(BF16)
    hgrads[:, 512:768] = odd[:, 256:512].astype(BF16)
    hgrads[:, 768:1024] = even[:, 256:512].astype(BF16)
    arrive(1)
    low = jnp.where(has_low, vlo[...].reshape(64, 1024), zero)
    high = jnp.where(has_high, vhi[...].reshape(64, 1024), zero)
    cells = jnp.concatenate([low, vol[...].reshape(64, 1024), high], axis=0)
    split = mm(cells, order[...])

    def volume_part(phase):
        return jnp.concatenate(
            [split[32 * p : 32 * p + 32, 256 * phase : 256 * phase + 256] for p in range(6)], axis=1
        )

    for index, part in enumerate(windows(volume_part, 1536, us)):
        t1[32 * index : 32 * index + 32, :] = part

    tn = ((0,), (0,))
    nt = ((1,), (1,))
    pre = mm(w1[0], t1[:, 0:1024], tn)
    pre += mm(w1[1], t1[:, 256:1280], tn)
    pre += mm(w1[2], t1[:, 512:1536], tn)
    sigma = 1.0 / (1.0 + jnp.exp(-pre))
    plane = lax.broadcasted_iota(jnp.int32, (1, 1024), 1) >> 8
    real = ((plane > 0) | has_low) & ((plane < 3) | has_high)
    hidden = jnp.where(real, pre * sigma, 0.0).astype(BF16).astype(F32)
    for index, part in enumerate(
        windows(lambda ph: hidden[64 * ph : 64 * ph + 64, 0:768], 768, (-1, 0, 1))
    ):
        t2[64 * index : 64 * index + 64, :] = part
    for dz in range(3):
        here = t2[:, 256 * dz : 256 * dz + 256]
        grads[576 * dz : 576 * dz + 576, :] = mm(here, og[...], nt).astype(BF16)
    first.pair()
    second.pair()

    total = jnp.zeros((128, 256), F32)
    for dz in range(3):
        here = t2[:, 256 * dz : 256 * dz + 256]
        total += mm(k2[9 * dz : 9 * dz + 9].reshape(576, 128), here, tn)
    layer[...] = total.astype(BF16)

    slope = hgrads[...].astype(F32) * sigma * (1.0 + pre * (1.0 - sigma))
    pre_grads = jnp.where(real, slope, 0.0).astype(BF16)
    pre_wide = pre_grads.astype(F32)

    first.first_level()
    second.first_level()

    pairs = {}
    for dz in range(3):
        here = mm(t1[:, 256 * dz + 256 : 256 * dz + 768], pre_grads[:, 256:768], nt)
        for dy in range(3):
            for dx in range(3):
                term = None
                for index, (py, px) in enumerate(phases):
                    row = 32 * (4 * (py + dy) + px + dx)
                    block = here[row : row + 32, 64 * index : 64 * index + 64]
                    term = block if term is None else term + block
                pairs[9 * dz + 3 * dy + dx] = term
    pairs[27] = jnp.zeros((32, 64), F32)
    for tap in range(PAIR):
        grads[ROWS_TWO + 32 * tap : ROWS_TWO + 32 * tap + 32, :] = jnp.concatenate(
            [pairs[tap], pairs[tap + PAIR]], axis=1
        ).astype(BF16)
    used = ROWS_TWO + ROWS_ONE
    if grads.shape[0] > used:
        grads[used:, :] = jnp.zeros((grads.shape[0] - used, 128), BF16)
    late.pair()

    for index, part in enumerate(
        windows(lambda ph: pre_wide[64 * ph : 64 * ph + 64, :], 1024, us)
    ):
        tg[64 * index : 64 * index + 64, :] = part
    late.first_level()

    back = mm(wc[0], tg[:, 512:1024]) + mm(wc[1], tg[:, 256:768]) + mm(wc[2], tg[:, 0:512])
    back = back.astype(BF16)
    for z in range(2):
        plane_rows = jnp.concatenate(
            [back[32 * ph : 32 * ph + 32, 256 * z : 256 * z + 256] for ph in range(4)], axis=1
        )
        igrads[z] = mm(plane_rows, order[...], nt).astype(BF16)

    for item in sums:
        item.second_level()
    for item in sums:
        item.second_back()
    for item in sums:
        item.first_back()
    for item in sums:
        item.pair_back()
    for item in sums:
        item.wait()


def tail_kernel(scale_one, scale_two, layer, igrads, summed, layer_out, igrads_out, first, second):
    layer_out[...] = layer[...]
    igrads_out[...] = igrads[...]
    second[...] = summed[0:ROWS_TWO, :].astype(F32) * scale_two
    for tap in range(27):
        start = ROWS_TWO + 32 * (tap % PAIR)
        block = summed[start : start + 32, :]
        half = block[:, 0:64] if tap < PAIR else block[:, 64:128]
        first[tap] = half.astype(F32) * scale_one


def local(volume, out_grads, kernel_one, kernel_two):
    spaces, samples = lax.axis_size("space"), lax.axis_size("sample")
    depth, batch, channels_in, plane = volume.shape
    scale_one = float(samples * batch * spaces * depth * plane) ** (-0.5)
    scale_two = scale_one * 8.0**0.5
    vol = volume.reshape(depth, channels_in, plane)
    og = out_grads.reshape(128, 256)
    chips, lines, streams = plan(samples, spaces)
    rows = streams[2][0] + streams[2][1]
    buffers = []
    for _, size, line_first in streams:
        outer, inner = (lines, chips) if line_first else (chips, lines)
        chunk, piece = level_rows(size, outer, inner)
        buffers += [
            pltpu.VMEM((size // 2, 128), BF16),
            pltpu.VMEM((size // 2, 128), BF16),
            pltpu.VMEM((outer, chunk, 128), BF16),
            pltpu.VMEM((inner * piece, 128), BF16),
            pltpu.VMEM((inner, piece, 128), BF16),
            pltpu.VMEM((inner * piece, 128), BF16),
        ]
    layer, igrads, summed = pl.pallas_call(
        functools.partial(whole_kernel, samples, spaces),
        out_shape=[
            jax.ShapeDtypeStruct((128, 256), BF16),
            jax.ShapeDtypeStruct((2, 32, 1024), BF16),
            jax.ShapeDtypeStruct((rows, 128), BF16),
        ],
        in_specs=[pl.BlockSpec(memory_space=pltpu.HBM)] * 4,
        out_specs=[VMEM_SPEC] * 3,
        scratch_shapes=[
            pltpu.VMEM(vol.shape, BF16),
            pltpu.VMEM(og.shape, BF16),
            pltpu.VMEM(kernel_one.shape, BF16),
            pltpu.VMEM(kernel_two.shape, BF16),
            pltpu.VMEM(vol.shape, BF16),
            pltpu.VMEM(vol.shape, BF16),
            pltpu.VMEM(og.shape, BF16),
            pltpu.VMEM(og.shape, BF16),
            pltpu.VMEM((rows, 128), BF16),
            pltpu.VMEM((1024, 1024), BF16),
            pltpu.VMEM((512, 1536), BF16),
            pltpu.VMEM((576, 768), BF16),
            pltpu.VMEM((512, 768), BF16),
            pltpu.VMEM((1024, 1024), BF16),
            pltpu.VMEM((3, 512, 256), BF16),
            pltpu.VMEM((3, 256, 512), BF16),
            pltpu.VMEM((3, 128, 1024), BF16),
            pltpu.VMEM((256, 1024), BF16),
            *buffers,
            pltpu.SemaphoreType.DMA((3, 2, 6, max(chips, lines))),
            pltpu.SemaphoreType.DMA((4,)),
            pltpu.SemaphoreType.DMA((2, 4)),
        ],
        compiler_params=pltpu.CompilerParams(
            collective_id=0, has_side_effects=True, vmem_limit_bytes=56 * 2**20
        ),
        name="conv_pair",
    )(vol, og, kernel_one, kernel_two)
    layer, igrads, first, second = pl.pallas_call(
        functools.partial(tail_kernel, scale_one, scale_two),
        out_shape=[
            jax.ShapeDtypeStruct(layer.shape, BF16),
            jax.ShapeDtypeStruct(igrads.shape, BF16),
            jax.ShapeDtypeStruct(kernel_one.shape, F32),
            jax.ShapeDtypeStruct((ROWS_TWO, 128), F32),
        ],
        in_specs=[VMEM_SPEC] * 3,
        out_specs=[VMEM_SPEC] * 4,
        compiler_params=pltpu.CompilerParams(vmem_limit_bytes=56 * 2**20),
        name="finish",
    )(layer, igrads, summed)
    return (
        layer.reshape(out_grads.shape),
        igrads.reshape(volume.shape),
        first,
        second.reshape(kernel_two.shape),
    )


def solution(mesh):
    in_specs = (P("space", "sample", None, None), P("space", "sample", None, None), P(), P())
    out_specs = (P("space", "sample", None, None), P("space", "sample", None, None), P(), P())
    return jax.shard_map(local, mesh=mesh, in_specs=in_specs, out_specs=out_specs, check_vma=False)
```

```python
import functools
import math

import jax
import jax.numpy as jnp
from jax import lax
from jax.experimental import pallas as pl
from jax.experimental.pallas import tpu as pltpu
from jax.sharding import PartitionSpec as P

F32 = jnp.float32
BF16 = jnp.bfloat16
MESH = pl.DeviceIdType.MESH
VMEM_SPEC = pl.BlockSpec(memory_space=pltpu.VMEM)
PAIR = 14
ROWS_TWO = 27 * 64
ROWS_ONE = PAIR * 32
WINDOWS = {-1: (1, -1), 0: (0, 0), 1: (1, 0), 2: (0, 1)}


def plan(samples, spaces):
    chips, lines = 2 * samples, spaces // 4
    unit = 32 * math.lcm(chips, lines)
    units = -(-(ROWS_TWO + ROWS_ONE) // unit)
    early = ROWS_TWO // unit
    cut = (early + 1) // 2
    bounds = [0, cut * unit, early * unit, units * unit]
    streams = [(bounds[n], bounds[n + 1] - bounds[n], n == 1) for n in range(3)]
    return chips, lines, streams


def level_rows(size, outer, inner):
    chunk = size // 2 // outer
    return chunk, -(-chunk // inner // 16) * 16


def mm(a, b, dims=((1,), (0,))):
    return lax.dot_general(a, b, (dims, ((), ())), preferred_element_type=F32)


def windows(parts, lanes, us):
    cell = lax.broadcasted_iota(jnp.int32, (1, lanes), 1)
    q, r = (cell >> 4) & 15, cell & 15
    for uy in us:
        for ux in us:
            (py, sy), (px, sx) = WINDOWS[uy], WINDOWS[ux]
            part = parts(2 * py + px)
            offset = 16 * sy + sx
            if offset != 0:
                part = pltpu.roll(part, (-offset) % lanes, 1)
                inside = (q + sy >= 0) & (q + sy <= 15) & (r + sx >= 0) & (r + sx <= 15)
                part = jnp.where(inside, part, 0.0)
            yield part.astype(BF16)


def tap_block(kernel, dz, dy, dx, shape):
    if 0 <= dy <= 2 and 0 <= dx <= 2:
        return kernel[9 * dz + 3 * dy + dx]
    return jnp.zeros(shape, BF16)


class Sum:
    def __init__(self, stream, samples, spaces, grads, out, bufs, sems):
        self.base, size, line_first = stream
        self.grads, self.out, self.sems = grads, out, sems
        self.slot, self.held, self.slots, self.part, self.far, self.done = bufs
        chips, lines = 2 * samples, spaces // 4
        sample, space = lax.axis_index("sample"), lax.axis_index("space")
        core, line = lax.rem(space, 2), space // 4
        chip = 2 * sample + lax.rem(space // 2, 2)
        self.core, self.half = core, size // 2
        self.sibling = (sample, space + 1 - 2 * core)
        others = [lax.rem(chip + d, chips) for d in range(chips)]
        ahead = [lax.rem(line + d, lines) for d in range(lines)]
        plane = (chip, others, [(c // 2, 4 * line + 2 * lax.rem(c, 2) + core) for c in others])
        column = (line, ahead, [(sample, 4 * n + lax.rem(space, 4)) for n in ahead])
        self.outer, self.inner = (column, plane) if line_first else (plane, column)
        self.chunk, self.piece = level_rows(size, len(self.outer[1]), len(self.inner[1]))

    def peers(self):
        return [self.sibling] + self.outer[2][1:] + self.inner[2][1:]

    def rows(self, start, size):
        return pl.ds(pl.multiple_of(start, 16), size)

    def send(self, stage, items):
        self.flying = []
        for d, (src, dst, target) in enumerate(items):
            copy = pltpu.make_async_remote_copy(
                src_ref=src,
                dst_ref=dst,
                send_sem=self.sems.at[0, stage, d],
                recv_sem=self.sems.at[1, stage, d],
                device_id=target,
                device_id_type=MESH,
            )
            copy.start()
            self.flying.append(copy)

    def wait(self):
        for copy in self.flying:
            copy.wait()

    def scatter(self, stage, level, source, size, slots):
        _, indices, peers = level
        items = []
        for d in range(1, len(peers)):
            src = source.at[self.rows(indices[d] * size, size)]
            items.append((src, slots.at[d], peers[d]))
        self.send(stage, items)

    def gathered(self, level, source, size, slots):
        total = source[self.rows(level[0] * size, size), :].astype(F32)
        for d in range(1, len(level[2])):
            total += slots[d].astype(F32)
        return total.astype(BF16)

    def pair(self):
        away = self.rows(self.base + (1 - self.core) * self.half, self.half)
        self.send(0, [(self.grads.at[away], self.slot, self.sibling)])

    def first_level(self):
        self.wait()
        own = self.grads[self.rows(self.base + self.core * self.half, self.half), :]
        self.held[...] = (own.astype(F32) + self.slot[...].astype(F32)).astype(BF16)
        self.scatter(1, self.outer, self.held, self.chunk, self.slots)

    def second_level(self):
        self.wait()
        self.part[0 : self.chunk, :] = self.gathered(self.outer, self.held, self.chunk, self.slots)
        extra = self.part.shape[0] - self.chunk
        if extra > 0:
            self.part[self.chunk :, :] = jnp.zeros((extra, 128), BF16)
        self.scatter(2, self.inner, self.part, self.piece, self.far)

    def second_back(self):
        self.wait()
        mine = self.rows(self.inner[0] * self.piece, self.piece)
        self.done[mine, :] = self.gathered(self.inner, self.part, self.piece, self.far)
        target = self.done.at[mine]
        self.send(3, [(target, target, peer) for peer in self.inner[2][1:]])

    def first_back(self):
        self.wait()
        start = self.base + self.core * self.half + self.outer[0] * self.chunk
        mine = self.rows(start, self.chunk)
        self.out[mine, :] = self.done[0 : self.chunk, :]
        target = self.out.at[mine]
        self.send(4, [(target, target, peer) for peer in self.outer[2][1:]])

    def pair_back(self):
        self.wait()
        target = self.out.at[self.rows(self.base + self.core * self.half, self.half)]
        self.send(5, [(target, target, self.sibling)])


def whole_kernel(
    samples, spaces, vol_far, og_far, k1_far, k2_far,
    layer, igrads, out,
    vol, og, k1, k2, vlo, vhi, olo, ohi, grads,
    order, t1, t2, o4, tg, w1, wb, wc, hgrads,
    *rest,
):
    sems, local_sems, halo_sems = rest[18:]
    me, sample = lax.axis_index("space"), lax.axis_index("sample")
    has_low, has_high = me > 0, me < spaces - 1
    below, above = me - 1, me + 1
    fetched = [
        pltpu.make_async_copy(src, dst, local_sems.at[n])
        for n, (src, dst) in enumerate(
            [(k1_far, k1), (k2_far, k2), (vol_far, vol), (og_far, og)]
        )
    ]
    for item in fetched:
        item.start()

    _, _, streams = plan(samples, spaces)
    sums = [
        Sum(stream, samples, spaces, grads, out, rest[6 * n : 6 * n + 6], sems.at[n])
        for n, stream in enumerate(streams)
    ]
    first, second, late = sums
    barrier = pltpu.get_barrier_semaphore()

    @pl.when(has_low)
    def _():
        pl.semaphore_signal(barrier, inc=1, device_id=(sample, below), device_id_type=MESH)

    @pl.when(has_high)
    def _():
        pl.semaphore_signal(barrier, inc=1, device_id=(sample, above), device_id_type=MESH)

    peers = first.peers()
    for peer in peers:
        pl.semaphore_signal(barrier, inc=1, device_id=peer, device_id_type=MESH)
    near = jnp.minimum(me, 1) + jnp.minimum(spaces - 1 - me, 1)
    pl.semaphore_wait(barrier, near + len(peers))

    def halo(src, dst, index, target):
        return pltpu.make_async_remote_copy(
            src_ref=src,
            dst_ref=dst,
            send_sem=halo_sems.at[0, index],
            recv_sem=halo_sems.at[1, index],
            device_id=(sample, target),
            device_id_type=MESH,
        )

    up = [(vol_far, vlo, 0), (og_far, olo, 1)]
    down = [
        (vol_far.at[0], vhi.at[0], 2),
        (og_far, ohi, 3),
        (vol_far.at[1], vhi.at[1], 4),
    ]

    @pl.when(has_high)
    def _():
        for src, dst, index in up:
            halo(src, dst, index, above).start()

    @pl.when(has_low)
    def _():
        for src, dst, index in down:
            halo(src, dst, index, below).start()

    def order_rows(step, carry):
        start = pl.multiple_of(step * 128, 128)
        col = lax.broadcasted_iota(jnp.int32, (1, 1024), 1)
        phase, q, r = col >> 8, (col >> 4) & 15, col & 15
        source = (2 * q + (phase >> 1)) * 32 + 2 * r + (phase & 1)
        row = lax.broadcasted_iota(jnp.int32, (128, 1024), 0) + start
        order[pl.ds(start, 128), :] = jnp.where(row == source, 1.0, 0.0).astype(BF16)
        return carry

    lax.fori_loop(0, 8, order_rows, 0)

    fetched[0].wait()
    fetched[1].wait()
    us = (-1, 0, 1, 2)
    phases = [(0, 0), (0, 1), (1, 0), (1, 1)]
    for dz in range(3):
        for index, (uy, ux) in enumerate((a, b) for a in us for b in us):
            w1[dz, 32 * index : 32 * index + 32, :] = jnp.concatenate(
                [tap_block(k1, dz, uy - py + 1, ux - px + 1, (32, 64)) for py, px in phases], axis=1
            )
        for index, (py, px) in enumerate(phases):
            wc[dz, 32 * index : 32 * index + 32, :] = jnp.concatenate(
                [tap_block(k1, dz, py + 1 - uy, px + 1 - ux, (32, 64)) for uy in us for ux in us],
                axis=1,
            )
            taps = {(0, 0): 1, (0, 1): -1, (1, 0): 2, (1, 1): 0}
            wb[dz, 64 * index : 64 * index + 64, :] = jnp.concatenate(
                [
                    tap_block(k2, dz, taps[py, sy], taps[px, sx], (64, 128))
                    for sy in (0, 1)
                    for sx in (0, 1)
                ],
                axis=1,
            )

    def arrive(ups, downs):
        @pl.when(has_high)
        def _():
            for src, dst, index in ups:
                halo(src, dst, index, above).wait_send()
            for src, dst, index in downs:
                halo(src, dst, index, above).wait_recv()

        @pl.when(has_low)
        def _():
            for src, dst, index in downs:
                halo(src, dst, index, below).wait_send()
            for src, dst, index in ups:
                halo(src, dst, index, below).wait_recv()

    fetched[2].wait()
    fetched[3].wait()
    arrive(up[:1], down[:1])
    zero = jnp.zeros((), BF16)
    low = jnp.where(has_low, vlo[...].reshape(64, 1024), zero)
    high = jnp.where(has_high, vhi[0], zero)
    cells = jnp.concatenate([low, vol[...].reshape(64, 1024), high], axis=0)
    split = mm(cells, order[...])

    def volume_part(phase):
        return jnp.concatenate(
            [split[32 * p : 32 * p + 32, 256 * phase : 256 * phase + 256] for p in range(5)], axis=1
        )

    for index, part in enumerate(windows(volume_part, 1280, us)):
        t1[32 * index : 32 * index + 32, 0:1280] = part

    tn = ((0,), (0,))
    nt = ((1,), (1,))
    pre = mm(w1[0], t1[:, 0:768], tn)
    pre += mm(w1[1], t1[:, 256:1024], tn)
    pre += mm(w1[2], t1[:, 512:1280], tn)
    sigma = 1.0 / (1.0 + jnp.exp(-pre))
    plane = lax.broadcasted_iota(jnp.int32, (1, 768), 1) >> 8
    hidden = jnp.where((plane > 0) | has_low, pre * sigma, 0.0).astype(BF16).astype(F32)
    for index, part in enumerate(
        windows(lambda ph: hidden[64 * ph : 64 * ph + 64, 0:768], 768, (-1, 0, 1))
    ):
        t2[64 * index : 64 * index + 64, :] = part
    for dz in range(3):
        here = t2[:, 256 * dz : 256 * dz + 256]
        grads[576 * dz : 576 * dz + 576, :] = mm(here, og[...], nt).astype(BF16)
    first.pair()
    second.pair()

    total = jnp.zeros((128, 256), F32)
    for dz in range(3):
        here = t2[:, 256 * dz : 256 * dz + 256]
        total += mm(k2[9 * dz : 9 * dz + 9].reshape(576, 128), here, tn)
    layer[...] = total.astype(BF16)

    first.first_level()
    second.first_level()

    arrive(up[1:], down[1:2])
    og_three = jnp.concatenate(
        [jnp.where(has_low, olo[...], zero), og[...], jnp.where(has_high, ohi[...], zero)], axis=1
    ).astype(F32)
    cell = lax.broadcasted_iota(jnp.int32, (1, 768), 1)
    q, r = (cell >> 4) & 15, cell & 15
    for sy in (0, 1):
        for sx in (0, 1):
            part = og_three
            if sy + sx > 0:
                part = pltpu.roll(part, 768 - 16 * sy - sx, 1)
                part = jnp.where((q + sy <= 15) & (r + sx <= 15), part, 0.0)
            index = 2 * sy + sx
            o4[128 * index : 128 * index + 128, :] = part.astype(BF16)

    even = mm(wb[1], o4[:, 256:768])
    odd = mm(wb[2], o4[:, 0:512]) + mm(wb[0], o4[:, 256:768])
    hgrads[:, 0:256] = odd[:, 0:256].astype(BF16)
    hgrads[:, 256:512] = even[:, 0:256].astype(BF16)
    hgrads[:, 512:768] = odd[:, 256:512].astype(BF16)
    hgrads[:, 768:1024] = even[:, 256:512].astype(BF16)

    slope = hgrads[:, 0:768].astype(F32) * sigma * (1.0 + pre * (1.0 - sigma))
    pre_grads = jnp.where((plane > 0) | has_low, slope, 0.0).astype(BF16)

    pairs = {}
    for dz in range(3):
        here = mm(t1[:, 256 * dz + 256 : 256 * dz + 768], pre_grads[:, 256:768], nt)
        for dy in range(3):
            for dx in range(3):
                term = None
                for index, (py, px) in enumerate(phases):
                    row = 32 * (4 * (py + dy) + px + dx)
                    block = here[row : row + 32, 64 * index : 64 * index + 64]
                    term = block if term is None else term + block
                pairs[9 * dz + 3 * dy + dx] = term
    pairs[27] = jnp.zeros((32, 64), F32)
    for tap in range(PAIR):
        grads[ROWS_TWO + 32 * tap : ROWS_TWO + 32 * tap + 32, :] = jnp.concatenate(
            [pairs[tap], pairs[tap + PAIR]], axis=1
        ).astype(BF16)
    used = ROWS_TWO + ROWS_ONE
    if grads.shape[0] > used:
        grads[used:, :] = jnp.zeros((grads.shape[0] - used, 128), BF16)
    late.pair()

    arrive([], down[2:])
    last = mm(jnp.where(has_high, vhi[1], zero), order[...])
    for index, part in enumerate(
        windows(lambda ph: last[:, 256 * ph : 256 * ph + 256], 256, us)
    ):
        t1[32 * index : 32 * index + 32, 1280:1536] = part
    pre_last = mm(w1[0], t1[:, 768:1024], tn)
    pre_last += mm(w1[1], t1[:, 1024:1280], tn)
    pre_last += mm(w1[2], t1[:, 1280:1536], tn)
    sigma_last = 1.0 / (1.0 + jnp.exp(-pre_last))
    slope = hgrads[:, 768:1024].astype(F32) * sigma_last * (1.0 + pre_last * (1.0 - sigma_last))
    slope = jnp.where(has_high, slope, 0.0).astype(BF16)
    pre_wide = jnp.concatenate([pre_grads, slope], axis=1).astype(F32)
    for index, part in enumerate(
        windows(lambda ph: pre_wide[64 * ph : 64 * ph + 64, :], 1024, us)
    ):
        tg[64 * index : 64 * index + 64, :] = part
    late.first_level()

    back = mm(wc[0], tg[:, 512:1024]) + mm(wc[1], tg[:, 256:768]) + mm(wc[2], tg[:, 0:512])
    back = back.astype(BF16)
    for z in range(2):
        plane_rows = jnp.concatenate(
            [back[32 * ph : 32 * ph + 32, 256 * z : 256 * z + 256] for ph in range(4)], axis=1
        )
        igrads[z] = mm(plane_rows, order[...], nt).astype(BF16)

    for item in sums:
        item.second_level()
    for item in sums:
        item.second_back()
    for item in sums:
        item.first_back()
    for item in sums:
        item.pair_back()
    for item in sums:
        item.wait()


def tail_kernel(scale_one, scale_two, layer, igrads, summed, layer_out, igrads_out, first, second):
    layer_out[...] = layer[...]
    igrads_out[...] = igrads[...]
    second[...] = summed[0:ROWS_TWO, :].astype(F32) * scale_two
    for tap in range(27):
        start = ROWS_TWO + 32 * (tap % PAIR)
        block = summed[start : start + 32, :]
        half = block[:, 0:64] if tap < PAIR else block[:, 64:128]
        first[tap] = half.astype(F32) * scale_one


def local(volume, out_grads, kernel_one, kernel_two):
    spaces, samples = lax.axis_size("space"), lax.axis_size("sample")
    depth, batch, channels_in, plane = volume.shape
    scale_one = float(samples * batch * spaces * depth * plane) ** (-0.5)
    scale_two = scale_one * 8.0**0.5
    vol = volume.reshape(depth, channels_in, plane)
    og = out_grads.reshape(128, 256)
    chips, lines, streams = plan(samples, spaces)
    rows = streams[2][0] + streams[2][1]
    buffers = []
    for _, size, line_first in streams:
        outer, inner = (lines, chips) if line_first else (chips, lines)
        chunk, piece = level_rows(size, outer, inner)
        buffers += [
            pltpu.VMEM((size // 2, 128), BF16),
            pltpu.VMEM((size // 2, 128), BF16),
            pltpu.VMEM((outer, chunk, 128), BF16),
            pltpu.VMEM((inner * piece, 128), BF16),
            pltpu.VMEM((inner, piece, 128), BF16),
            pltpu.VMEM((inner * piece, 128), BF16),
        ]
    layer, igrads, summed = pl.pallas_call(
        functools.partial(whole_kernel, samples, spaces),
        out_shape=[
            jax.ShapeDtypeStruct((128, 256), BF16),
            jax.ShapeDtypeStruct((2, 32, 1024), BF16),
            jax.ShapeDtypeStruct((rows, 128), BF16),
        ],
        in_specs=[pl.BlockSpec(memory_space=pltpu.HBM)] * 4,
        out_specs=[VMEM_SPEC] * 3,
        scratch_shapes=[
            pltpu.VMEM(vol.shape, BF16),
            pltpu.VMEM(og.shape, BF16),
            pltpu.VMEM(kernel_one.shape, BF16),
            pltpu.VMEM(kernel_two.shape, BF16),
            pltpu.VMEM(vol.shape, BF16),
            pltpu.VMEM(vol.shape, BF16),
            pltpu.VMEM(og.shape, BF16),
            pltpu.VMEM(og.shape, BF16),
            pltpu.VMEM((rows, 128), BF16),
            pltpu.VMEM((1024, 1024), BF16),
            pltpu.VMEM((512, 1536), BF16),
            pltpu.VMEM((576, 768), BF16),
            pltpu.VMEM((512, 768), BF16),
            pltpu.VMEM((1024, 1024), BF16),
            pltpu.VMEM((3, 512, 256), BF16),
            pltpu.VMEM((3, 256, 512), BF16),
            pltpu.VMEM((3, 128, 1024), BF16),
            pltpu.VMEM((256, 1024), BF16),
            *buffers,
            pltpu.SemaphoreType.DMA((3, 2, 6, max(chips, lines))),
            pltpu.SemaphoreType.DMA((4,)),
            pltpu.SemaphoreType.DMA((2, 5)),
        ],
        compiler_params=pltpu.CompilerParams(
            collective_id=0, has_side_effects=True, vmem_limit_bytes=56 * 2**20
        ),
        name="conv_pair",
    )(vol, og, kernel_one, kernel_two)
    layer, igrads, first, second = pl.pallas_call(
        functools.partial(tail_kernel, scale_one, scale_two),
        out_shape=[
            jax.ShapeDtypeStruct(layer.shape, BF16),
            jax.ShapeDtypeStruct(igrads.shape, BF16),
            jax.ShapeDtypeStruct(kernel_one.shape, F32),
            jax.ShapeDtypeStruct((ROWS_TWO, 128), F32),
        ],
        in_specs=[VMEM_SPEC] * 3,
        out_specs=[VMEM_SPEC] * 4,
        compiler_params=pltpu.CompilerParams(vmem_limit_bytes=56 * 2**20),
        name="finish",
    )(layer, igrads, summed)
    return (
        layer.reshape(out_grads.shape),
        igrads.reshape(volume.shape),
        first,
        second.reshape(kernel_two.shape),
    )


def solution(mesh):
    in_specs = (P("space", "sample", None, None), P("space", "sample", None, None), P(), P())
    out_specs = (P("space", "sample", None, None), P("space", "sample", None, None), P(), P())
    return jax.shard_map(local, mesh=mesh, in_specs=in_specs, out_specs=out_specs, check_vma=False)
```
